128 devices in a mesh: row: 16 (over x_lo, y, core), col: 8 (over x_hi, z).
Axes of the slice: x: 4 (x_hi: 2, x_lo: 2; x = x_hi * 2 + x_lo), y: 4, z: 4, core: 2. Of those that a mesh axis runs over, the one named last changes fastest.
Arguments:
- features: bfloat16 [16384, 1408], P(('row', 'col')), may hold values from -8 to 8
- proj_weight: bfloat16 [1408, 1024], replicated, may hold values from -1.5 to 1.5
- image_vals: bfloat16 [16384, 1024], P(('row', 'col')), may hold values from -1 to 1
- image_scales: bfloat16 [16384, 8], P(('row', 'col')), may hold values from 0.05 to 1
- text_vals: bfloat16 [16384, 1024], P(('row', 'col')), may hold values from -1 to 1
- text_scales: bfloat16 [16384, 8], P(('row', 'col')), may hold values from 0.05 to 1
- logit_scale: float32 [1], replicated, may hold values from 30 to 180
Outputs:
- loss: float32 [], replicated
- grad_w: float32 [1408, 1024], replicated
The draws below stay inside these ranges and needn't reach their ends.
All inputs are finite; a program needn't handle non-finite values.
Results may differ from the reference program's by a relative error of at most 0.0003.
The reference program's roundings to bfloat16 on the way (of `point_unit`) count: a program that leaves them out, or rounds other values in their place, can miss the bound.
Values may be sent and summed in bfloat16 or wider, within the bound.
No kernel may reach another device: no remote copies, remote signals or barrier semaphores. Data moves between devices by JAX's collectives and lax.ppermute only.
A program may use at most 128 MiB of HBM per device.

```python
import math
import jax
import jax.numpy as jnp
from jax import lax

E = 1408
C = 1024
QB = 128
BATCH = 16384


def row_layout(base_key):
    layout_key = jax.random.fold_in(base_key, 101)
    sub_keys = jax.random.split(layout_key, 5)
    pair_kind = jax.random.randint(sub_keys[0], (BATCH // 2,), 0, 8)
    row_kind = jnp.repeat(pair_kind, 2)
    leading = jnp.arange(BATCH) % 2 == 0
    aligned = (row_kind == 0)[:, None]
    anti_point = ((row_kind == 1) & leading)[:, None]
    anti_target = ((row_kind == 1) & jnp.logical_not(leading))[:, None]
    directions = (jax.random.randint(sub_keys[1], (4, C), 0, 2) * 2 - 1).astype(jnp.float32) / math.sqrt(C)
    shared = jnp.repeat(jax.random.normal(sub_keys[2], (BATCH // 2, C), jnp.float32), 2, axis=0) / math.sqrt(C)
    spread = jnp.repeat(jnp.exp(jax.random.uniform(sub_keys[3], (BATCH // 2,), jnp.float32, math.log(0.15), math.log(0.45))), 2)[:, None]
    single = jax.random.normal(sub_keys[4], (BATCH, C), jnp.float32) / math.sqrt(C)
    return (aligned, anti_point, anti_target, directions, shared, spread, single)


def target_design(base_key, layout, which):
    aligned, anti_point, anti_target, directions, shared, spread, single = layout
    fresh = jax.random.normal(jax.random.fold_in(base_key, 200 + which), (BATCH, C), jnp.float32) / math.sqrt(C)
    drawn = fresh
    matched = fresh
    opposed = fresh
    return jnp.where(aligned, matched, jnp.where(anti_target, opposed, drawn))


def target_blocks(base_key, which, block_low):
    layout = row_layout(base_key)
    design = target_design(base_key, layout, which)
    gain_key = jax.random.fold_in(base_key, 300 + which)
    row_key, block_key = jax.random.split(gain_key)
    row_gain = jnp.exp(jax.random.uniform(row_key, (BATCH, 1, 1), jnp.float32, math.log(0.6), math.log(6.5)))
    block_gain = jnp.exp(jax.random.uniform(block_key, (BATCH, C // QB, 1), jnp.float32, math.log(block_low), 0.0))
    whole_rows = design.reshape(BATCH, C // QB, QB) * row_gain * block_gain
    block_peak = jnp.max(jnp.abs(whole_rows), axis=2, keepdims=True)
    scales = jnp.clip(block_peak, 0.05, 1.0)
    values = jnp.clip(whole_rows / scales, -1.0, 1.0)
    return (values.reshape(BATCH, C), scales.reshape(BATCH, C // QB))


def draw_features(key, part):
    key = jax.random.fold_in(key, 11)
    bound_abs = 6.0
    noise_draw = jax.random.normal(key, (BATCH, E), jnp.float32)
    lead_cols = noise_draw[:, :C]
    whole_rows = jnp.concatenate([lead_cols, noise_draw[:, C:]], axis=1)
    return jnp.clip(whole_rows, -bound_abs, bound_abs).astype(jnp.bfloat16)


def draw_proj_weight(key, part):
    key = jax.random.fold_in(key, 12)
    noise_draw = jax.random.normal(key, (E, C), jnp.float32) / math.sqrt(E)
    matrix = noise_draw
    return jnp.clip(matrix, -1.5, 1.5).astype(jnp.bfloat16)


def draw_image_vals(key, part):
    base_key = key
    block_low = 0.1
    values, scales = target_blocks(base_key, 1, block_low)
    return values.astype(jnp.bfloat16)


def draw_image_scales(key, part):
    base_key = key
    block_low = 0.1
    values, scales = target_blocks(base_key, 1, block_low)
    return scales.astype(jnp.bfloat16)


def draw_text_vals(key, part):
    base_key = key
    block_low = 0.1
    values, scales = target_blocks(base_key, 2, block_low)
    return values.astype(jnp.bfloat16)


def draw_text_scales(key, part):
    base_key = key
    block_low = 0.1
    values, scales = target_blocks(base_key, 2, block_low)
    return scales.astype(jnp.bfloat16)


def draw_logit_scale(key, part):
    key = jax.random.fold_in(key, 17)
    low_end, high_end = (30.0, 100.0)
    return jax.random.uniform(key, (1,), jnp.float32, low_end, high_end)


def setup_inputs(seed: int = 0) -> dict:
    arg_keys = jax.random.split(jax.random.key(seed), 8)
    return {
        "features": draw_features(jax.random.fold_in(arg_keys[7], 71), 0),
        "proj_weight": draw_proj_weight(jax.random.fold_in(arg_keys[7], 71), 0),
        "image_vals": draw_image_vals(jax.random.fold_in(arg_keys[7], 71), 0),
        "image_scales": draw_image_scales(jax.random.fold_in(arg_keys[7], 71), 0),
        "text_vals": draw_text_vals(jax.random.fold_in(arg_keys[7], 71), 0),
        "text_scales": draw_text_scales(jax.random.fold_in(arg_keys[7], 71), 0),
        "logit_scale": draw_logit_scale(jax.random.fold_in(arg_keys[7], 71), 0),
    }


EPS = 1e-06

def dequant(vals, scales):
    count = vals.shape[0]
    blocks = scales.shape[1]
    full = vals.astype(jnp.float32).reshape(count, blocks, vals.shape[1] // blocks)
    return (full * scales.astype(jnp.float32)[:, :, None]).reshape(count, vals.shape[1])

def unit_rows(full):
    return full * lax.rsqrt(lax.optimization_barrier(jnp.sum(full * full, axis=-1, keepdims=True)) + EPS)

def block_logits(points, image_unit, text_unit, scale):
    dims = (((1,), (1,)), ((), ()))
    first = lax.dot_general(points, image_unit, dims, preferred_element_type=jnp.float32)
    second = lax.dot_general(points, text_unit, dims, preferred_element_type=jnp.float32)
    return jnp.stack([first, second]) * scale

def reference(features, proj_weight, image_vals, image_scales, text_vals, text_scales, logit_scale):
    scale = logit_scale[0]
    proj = jnp.dot(features, proj_weight, preferred_element_type=jnp.float32)
    inv = lax.rsqrt(lax.optimization_barrier(jnp.sum(proj * proj, axis=-1, keepdims=True)) + EPS)
    point_unit = (proj * inv).astype(jnp.bfloat16)
    image_unit = unit_rows(dequant(image_vals, image_scales)).astype(jnp.bfloat16)
    text_unit = unit_rows(dequant(text_vals, text_scales)).astype(jnp.bfloat16)
    point_wide = point_unit.astype(jnp.float32)
    diag = scale * jnp.stack([lax.optimization_barrier(jnp.sum(point_wide * image_unit.astype(jnp.float32), axis=-1)), lax.optimization_barrier(jnp.sum(point_wide * text_unit.astype(jnp.float32), axis=-1))])
    total = point_unit.shape[0]
    step_rows = math.gcd(total, 1024)
    nblocks = total // step_rows
    point_blocks = point_unit.reshape(nblocks, step_rows, point_unit.shape[1])

    def first_pass(carry, points):
        col_max, col_sum = carry
        logits = block_logits(points, image_unit, text_unit, scale)
        row_max = lax.optimization_barrier(jnp.max(logits, axis=2))
        row_lse = row_max + jnp.log(lax.optimization_barrier(jnp.sum(jnp.exp(logits - row_max[:, :, None]), axis=2)))
        new_max = jnp.maximum(col_max, lax.optimization_barrier(jnp.max(logits, axis=1)))
        new_sum = col_sum * jnp.exp(col_max - new_max) + lax.optimization_barrier(jnp.sum(jnp.exp(logits - new_max[:, None, :]), axis=1))
        return ((new_max, new_sum), row_lse)
    start_max = jnp.full((2, total), -jnp.inf, jnp.float32)
    start_sum = jnp.zeros((2, total), jnp.float32)
    (col_max, col_sum), row_parts = lax.scan(first_pass, (start_max, start_sum), point_blocks)
    col_lse = col_max + jnp.log(col_sum)
    row_lse = jnp.transpose(row_parts, (1, 0, 2)).reshape(2, total)
    loss = (jnp.sum(row_lse) + jnp.sum(col_lse) - 2.0 * jnp.sum(diag)) / (4.0 * total)

    def second_pass(index):
        points = lax.dynamic_slice_in_dim(point_unit, index * step_rows, step_rows, 0)
        logits = block_logits(points, image_unit, text_unit, scale)
        lse_rows = lax.dynamic_slice_in_dim(row_lse, index * step_rows, step_rows, 1)
        rows_at = lax.broadcasted_iota(jnp.int32, (step_rows, total), 0) + (index * step_rows).astype(jnp.int32)
        cols_at = lax.broadcasted_iota(jnp.int32, (step_rows, total), 1)
        eye = jnp.where(rows_at == cols_at, 2.0, 0.0).astype(jnp.float32)
        coef = (jnp.exp(logits - lse_rows[:, :, None]) + jnp.exp(logits - col_lse[:, None, :]) - eye[None]).astype(jnp.bfloat16)
        return scale * 0.25 * (jnp.dot(coef[0], image_unit, preferred_element_type=jnp.float32) + jnp.dot(coef[1], text_unit, preferred_element_type=jnp.float32))
    point_grad = lax.map(second_pass, jnp.arange(nblocks, dtype=jnp.int32)).reshape(total, proj.shape[1])
    along = lax.optimization_barrier(jnp.sum(proj * point_grad, axis=-1, keepdims=True))
    proj_grad = inv * (point_grad - along * inv * inv * proj)
    grad_w = lax.dot_general(features.astype(jnp.float32), proj_grad, (((0,), (0,)), ((), ())), precision=lax.Precision.HIGHEST, preferred_element_type=jnp.float32)
    return (loss, grad_w)
```

```python
import jax
import jax.numpy as jnp
from jax import lax
from jax.sharding import PartitionSpec as P

EPS = 1e-06
AXES = ("row", "col")
X_POINT = (1, 0, 3, 2)
X_TARGET = (3, 2, 1, 0)


def device_index(x, y, z, core):
    row = ((x % 2) * 4 + y % 4) * 2 + core
    col = (x // 2) * 4 + z % 4
    return row * 8 + col


def take_from(value, x_map=None, dy=0, dz=0, flip=0):
    perm = []
    for x in range(4):
        source_x = x if x_map is None else x_map[x]
        for y in range(4):
            for z in range(4):
                for core in range(2):
                    source = device_index(source_x, y + dy, z + dz, core ^ flip)
                    perm.append((source, device_index(x, y, z, core)))
    return lax.ppermute(value, AXES, perm)


def gather_group(own, x_map, axis):
    def from_x(value):
        return take_from(value, x_map=x_map)

    def from_step(value, step):
        return take_from(value, **{axis: step})

    count = own.shape[0]
    cut = (count // 3) // 16 * 16
    near_x = from_x(own)
    after = from_step(own, 1)
    before = from_step(own, -1)
    x_before = from_step(near_x, -1)
    far = from_step(after, 1)
    x_after = from_x(after)
    x_far = jnp.concatenate(
        [
            from_step(x_before[:cut], -1),
            from_step(x_after[cut : 2 * cut], 1),
            from_x(far[2 * cut :]),
        ],
        axis=0,
    )
    return [[own, after, far, before], [near_x, x_after, x_far, x_before]]


def dequant(vals, scales):
    count = vals.shape[0]
    blocks = scales.shape[1]
    full = vals.astype(jnp.float32).reshape(count, blocks, vals.shape[1] // blocks)
    return (full * scales.astype(jnp.float32)[:, :, None]).reshape(count, vals.shape[1])


def unit_rows(full):
    return full * lax.rsqrt(jnp.sum(full * full, axis=-1, keepdims=True) + EPS)


def merged(parts):
    stack = jnp.stack(parts)
    top = jnp.max(stack, axis=0)
    return top + jnp.log(jnp.sum(jnp.exp(stack - top), axis=0))


def row_exchange(local):
    rows = local.shape[1] // 8
    parts = [local]
    for flip in range(2):
        for step in range(4):
            if flip or step:
                got = take_from(local, x_map=X_POINT if flip else None, dz=step)
                got = got.reshape(2, 2, 4, rows)
                if flip:
                    got = got[:, ::-1]
                parts.append(jnp.roll(got, step, axis=2).reshape(local.shape))
    return merged(parts)


def col_exchange(local):
    rows = local.shape[1] // 16
    parts = [local]
    for core in range(2):
        for flip in range(2):
            for step in range(4):
                if core or flip or step:
                    got = take_from(local, x_map=X_TARGET if flip else None, dy=step, flip=core)
                    got = got.reshape(2, 2, 2, 4, rows)
                    if core:
                        got = got[:, ::-1]
                    if flip:
                        got = got[:, :, ::-1]
                    parts.append(jnp.roll(got, step, axis=3).reshape(local.shape))
    return merged(parts)


def body(features, proj_weight, image_vals, image_scales, text_vals, text_scales, logit_scale):
    rows = features.shape[0]
    scale = logit_scale[0]
    total = rows * lax.axis_size("row") * lax.axis_size("col")
    image_own = unit_rows(dequant(image_vals, image_scales)).astype(jnp.bfloat16)
    text_own = unit_rows(dequant(text_vals, text_scales)).astype(jnp.bfloat16)
    target_own = jnp.concatenate([image_own, text_own], axis=0)

    point_blocks = gather_group(features, X_POINT, "dz")
    features_tile = jnp.concatenate(point_blocks[0] + point_blocks[1], axis=0)
    target_blocks = gather_group(target_own, X_TARGET, "dy")
    near = target_blocks[0] + target_blocks[1]
    other = [take_from(block, flip=1) for block in near]
    targets = near + other
    image_tile = jnp.concatenate([block[:rows] for block in targets], axis=0)
    text_tile = jnp.concatenate([block[rows:] for block in targets], axis=0)

    dims = (((1,), (1,)), ((), ()))
    proj = jnp.dot(features_tile, proj_weight, preferred_element_type=jnp.float32)
    inv = lax.rsqrt(jnp.sum(proj * proj, axis=-1, keepdims=True) + EPS)
    point_unit = (proj * inv).astype(jnp.bfloat16)
    first = lax.dot_general(point_unit, image_tile, dims, preferred_element_type=jnp.float32)
    second = lax.dot_general(point_unit, text_tile, dims, preferred_element_type=jnp.float32)
    logits = jnp.stack([first, second]) * scale
    point_wide = point_unit[:rows].astype(jnp.float32)
    diag = scale * jnp.stack(
        [
            jnp.sum(point_wide * image_own.astype(jnp.float32), axis=-1),
            jnp.sum(point_wide * text_own.astype(jnp.float32), axis=-1),
        ]
    )
    row_max = jnp.max(logits, axis=2)
    row_part = row_max + jnp.log(jnp.sum(jnp.exp(logits - row_max[:, :, None]), axis=2))
    col_max = jnp.max(logits, axis=1)
    col_part = col_max + jnp.log(jnp.sum(jnp.exp(logits - col_max[:, None, :]), axis=1))
    row_lse = row_exchange(row_part)
    col_lse = col_exchange(col_part)
    local_loss = jnp.sum(row_lse[:, :rows]) + jnp.sum(col_lse[:, :rows]) - 2.0 * jnp.sum(diag)

    tile_shape = (logits.shape[1], logits.shape[2])
    rows_at = lax.broadcasted_iota(jnp.int32, tile_shape, 0)
    cols_at = lax.broadcasted_iota(jnp.int32, tile_shape, 1)
    eye = jnp.where((rows_at == cols_at) & (rows_at < rows), 2.0, 0.0).astype(jnp.float32)
    coef = (
        jnp.exp(logits - row_lse[:, :, None]) + jnp.exp(logits - col_lse[:, None, :]) - eye[None]
    ).astype(jnp.bfloat16)
    point_grad = (scale * 0.25) * (
        jnp.dot(coef[0], image_tile, preferred_element_type=jnp.float32)
        + jnp.dot(coef[1], text_tile, preferred_element_type=jnp.float32)
    )
    along = jnp.sum(proj * point_grad, axis=-1, keepdims=True)
    proj_grad = inv * (point_grad - along * inv * inv * proj)
    high = lax.reduce_precision(proj_grad, 8, 7)
    low = (proj_grad - high).astype(jnp.bfloat16)
    high = high.astype(jnp.bfloat16)
    contract_rows = (((0,), (0,)), ((), ()))
    partial_w = lax.dot_general(
        features_tile, high, contract_rows, preferred_element_type=jnp.float32
    ) + lax.dot_general(features_tile, low, contract_rows, preferred_element_type=jnp.float32)
    loss_row = jnp.full((8, partial_w.shape[1]), local_loss, jnp.float32)
    summed = lax.psum(jnp.concatenate([partial_w, loss_row], axis=0), AXES)
    return (summed[-1, 0] / (4.0 * total), summed[:-8])


def solution(mesh):
    return jax.shard_map(
        body,
        mesh=mesh,
        in_specs=(
            P(("row", "col"), None),
            P(),
            P(("row", "col"), None),
            P(("row", "col"), None),
            P(("row", "col"), None),
            P(("row", "col"), None),
            P(),
        ),
        out_specs=(P(), P()),
        check_vma=False,
    )
```

```python
import jax
import jax.numpy as jnp
from jax import lax
from jax.sharding import PartitionSpec as P

EPS = 1e-06
AXES = ("row", "col")
X_POINT = (1, 0, 3, 2)
X_TARGET = (3, 2, 1, 0)


def device_index(x, y, z, core):
    row = ((x % 2) * 4 + y % 4) * 2 + core
    col = (x // 2) * 4 + z % 4
    return row * 8 + col


def take_from(value, x_map=None, dy=0, dz=0, flip=0):
    perm = []
    for x in range(4):
        source_x = x if x_map is None else x_map[x]
        for y in range(4):
            for z in range(4):
                for core in range(2):
                    source = device_index(source_x, y + dy, z + dz, core ^ flip)
                    perm.append((source, device_index(x, y, z, core)))
    return lax.ppermute(value, AXES, perm)


def gather_group(own, x_map, axis):
    def from_x(value):
        return take_from(value, x_map=x_map)

    def from_step(value, step):
        return take_from(value, **{axis: step})

    count = own.shape[0]
    cut = (count // 3) // 16 * 16
    near_x = from_x(own)
    after = from_step(own, 1)
    before = from_step(own, -1)
    x_before = from_step(near_x, -1)
    far = from_step(after, 1)
    x_after = from_x(after)
    x_far = jnp.concatenate(
        [
            from_step(x_before[:cut], -1),
            from_step(x_after[cut : 2 * cut], 1),
            from_x(far[2 * cut :]),
        ],
        axis=0,
    )
    return [[own, after, far, before], [near_x, x_after, x_far, x_before]]


def dequant(vals, scales):
    count = vals.shape[0]
    blocks = scales.shape[1]
    full = vals.astype(jnp.float32).reshape(count, blocks, vals.shape[1] // blocks)
    return (full * scales.astype(jnp.float32)[:, :, None]).reshape(count, vals.shape[1])


def unit_rows(full):
    return full * lax.rsqrt(jnp.sum(full * full, axis=-1, keepdims=True) + EPS)


def merged(parts):
    stack = jnp.stack(parts)
    top = jnp.max(stack, axis=0)
    return top + jnp.log(jnp.sum(jnp.exp(stack - top), axis=0))


def point_group(x, y, z, core):
    return (x // 2, y, core), (x % 2, z)


def target_group(x, y, z, core):
    pair = 0 if x in (0, 3) else 1
    return (pair, z), (core, 1 if x >= 2 else 0, y)


def same_core_group(x, y, z, core):
    return (core,), (x, y, z)


def groups_of(rule):
    found = {}
    for x in range(4):
        for y in range(4):
            for z in range(4):
                for core in range(2):
                    group, place = rule(x, y, z, core)
                    found.setdefault(group, []).append((place, device_index(x, y, z, core)))
    return [[device for _, device in sorted(found[group])] for group in sorted(found)]


def swap_blocks(value, rule):
    return lax.all_to_all(
        value, AXES, split_axis=0, concat_axis=0, axis_index_groups=groups_of(rule), tiled=True
    )


def rolled(value, shift, axis):
    out = value
    for step in range(1, 4):
        out = jnp.where(shift == step, jnp.roll(value, step, axis=axis), out)
    return out


def flipped(value, flag, axis):
    return jnp.where(flag == 1, jnp.flip(value, axis), value)


def merged(stack):
    top = jnp.max(stack, axis=0)
    return top + jnp.log(jnp.sum(jnp.exp(stack - top), axis=0))


def row_exchange(local, flip, z):
    rows = local.shape[1] // 8
    placed = rolled(flipped(local.reshape(2, 2, 4, rows), flip, 1), z, 2).reshape(local.shape)
    parts = swap_blocks(jnp.broadcast_to(placed, (8,) + placed.shape), point_group)
    whole = merged(parts).reshape(2, 2, 4, rows)
    return flipped(rolled(whole, (4 - z) % 4, 2), flip, 1).reshape(local.shape)


def col_exchange(local, core, flip, y):
    rows = local.shape[1] // 16
    placed = local.reshape(2, 2, 2, 4, rows)
    placed = rolled(flipped(flipped(placed, core, 1), flip, 2), y, 3).reshape(local.shape)
    parts = swap_blocks(jnp.broadcast_to(placed, (16,) + placed.shape), target_group)
    whole = merged(parts).reshape(2, 2, 2, 4, rows)
    return flipped(flipped(rolled(whole, (4 - y) % 4, 3), flip, 2), core, 1).reshape(local.shape)


def total_sum(partial, local_loss, core):
    high, wide = partial.shape
    cut = high // 16
    pieces = partial.reshape(2, 8, cut, 8, wide // 8).transpose(0, 1, 3, 2, 4)
    pieces = pieces.reshape(2, 64, cut, wide // 8)
    tail = jnp.full((2, 64, 8, wide // 8), local_loss, jnp.float32)
    pieces = jnp.concatenate([pieces, tail], axis=2)
    kept = lax.dynamic_index_in_dim(pieces, core, 0, False)
    sent = lax.dynamic_index_in_dim(pieces, 1 - core, 0, False)
    half = kept + take_from(sent, flip=1)
    own = jnp.sum(swap_blocks(half, same_core_group), axis=0)
    loss = own[cut, 0]
    here = swap_blocks(jnp.broadcast_to(own[:cut], (64, cut, wide // 8)), same_core_group)
    there = take_from(here, flip=1)
    both = jnp.where(core == 0, jnp.stack([here, there]), jnp.stack([there, here]))
    both = both.reshape(2, 8, 8, cut, wide // 8).transpose(0, 1, 3, 2, 4)
    return both.reshape(high, wide), loss


def body(features, proj_weight, image_vals, image_scales, text_vals, text_scales, logit_scale):
    rows = features.shape[0]
    scale = logit_scale[0]
    total = rows * lax.axis_size("row") * lax.axis_size("col")
    image_own = unit_rows(dequant(image_vals, image_scales)).astype(jnp.bfloat16)
    text_own = unit_rows(dequant(text_vals, text_scales)).astype(jnp.bfloat16)
    target_own = jnp.concatenate([image_own, text_own], axis=0)

    point_blocks = gather_group(features, X_POINT, "dz")
    features_tile = jnp.concatenate(point_blocks[0] + point_blocks[1], axis=0)
    target_blocks = gather_group(target_own, X_TARGET, "dy")
    near = target_blocks[0] + target_blocks[1]
    other = [take_from(block, flip=1) for block in near]
    targets = near + other
    image_tile = jnp.concatenate([block[:rows] for block in targets], axis=0)
    text_tile = jnp.concatenate([block[rows:] for block in targets], axis=0)

    dims = (((1,), (1,)), ((), ()))
    proj = jnp.dot(features_tile, proj_weight, preferred_element_type=jnp.float32)
    inv = lax.rsqrt(jnp.sum(proj * proj, axis=-1, keepdims=True) + EPS)
    point_unit = (proj * inv).astype(jnp.bfloat16)
    first = lax.dot_general(point_unit, image_tile, dims, preferred_element_type=jnp.float32)
    second = lax.dot_general(point_unit, text_tile, dims, preferred_element_type=jnp.float32)
    logits = jnp.stack([first, second]) * scale
    point_wide = point_unit[:rows].astype(jnp.float32)
    diag = scale * jnp.stack(
        [
            jnp.sum(point_wide * image_own.astype(jnp.float32), axis=-1),
            jnp.sum(point_wide * text_own.astype(jnp.float32), axis=-1),
        ]
    )
    row_max = jnp.max(logits, axis=2)
    row_part = row_max + jnp.log(jnp.sum(jnp.exp(logits - row_max[:, :, None]), axis=2))
    col_max = jnp.max(logits, axis=1)
    col_part = col_max + jnp.log(jnp.sum(jnp.exp(logits - col_max[:, None, :]), axis=1))
    row_index = lax.axis_index("row")
    col_index = lax.axis_index("col")
    x = (col_index // 4) * 2 + row_index // 8
    y = (row_index // 2) % 4
    z = col_index % 4
    core = row_index % 2
    row_lse = row_exchange(row_part, x % 2, z)
    col_lse = col_exchange(col_part, core, x // 2, y)
    local_loss = jnp.sum(row_lse[:, :rows]) + jnp.sum(col_lse[:, :rows]) - 2.0 * jnp.sum(diag)

    tile_shape = (logits.shape[1], logits.shape[2])
    rows_at = lax.broadcasted_iota(jnp.int32, tile_shape, 0)
    cols_at = lax.broadcasted_iota(jnp.int32, tile_shape, 1)
    eye = jnp.where((rows_at == cols_at) & (rows_at < rows), 2.0, 0.0).astype(jnp.float32)
    coef = (
        jnp.exp(logits - row_lse[:, :, None]) + jnp.exp(logits - col_lse[:, None, :]) - eye[None]
    ).astype(jnp.bfloat16)
    point_grad = (scale * 0.25) * (
        jnp.dot(coef[0], image_tile, preferred_element_type=jnp.float32)
        + jnp.dot(coef[1], text_tile, preferred_element_type=jnp.float32)
    )
    along = jnp.sum(proj * point_grad, axis=-1, keepdims=True)
    proj_grad = inv * (point_grad - along * inv * inv * proj)
    high = lax.reduce_precision(proj_grad, 8, 7)
    low = (proj_grad - high).astype(jnp.bfloat16)
    high = high.astype(jnp.bfloat16)
    contract_rows = (((0,), (0,)), ((), ()))
    partial_w = lax.dot_general(
        features_tile, high, contract_rows, preferred_element_type=jnp.float32
    ) + lax.dot_general(features_tile, low, contract_rows, preferred_element_type=jnp.float32)
    grad_w, loss = total_sum(partial_w, local_loss, core)
    return (loss / (4.0 * total), grad_w)


def solution(mesh):
    return jax.shard_map(
        body,
        mesh=mesh,
        in_specs=(
            P(("row", "col"), None),
            P(),
            P(("row", "col"), None),
            P(("row", "col"), None),
            P(("row", "col"), None),
            P(("row", "col"), None),
            P(),
        ),
        out_specs=(P(), P()),
        check_vma=False,
    )
```

```python
import functools
import jax
import jax.numpy as jnp
from jax import lax
from jax.experimental import pallas as pl
from jax.experimental.pallas import tpu as pltpu
from jax.sharding import PartitionSpec as P

EPS = 1e-06
LOG2E = 1.4426950408889634
LN2 = 0.6931471805599453
AXES = ("row", "col")
X_POINT = (1, 0, 3, 2)
X_TARGET = (3, 2, 1, 0)
VMEM_LIMIT = 58 * 1024 * 1024
LANES = 128
WIDE = 2 * LANES
BATCHES = (((0, 0), (1, 0), (0, 1), (0, 3)), ((1, 3), (0, 2), (1, 1)), ((1, 2),))
ORDER = [(core,) + place for batch in BATCHES for core in range(2) for place in batch]


def device_index(x, y, z, core):
    row = ((x % 2) * 4 + y % 4) * 2 + core
    col = (x // 2) * 4 + z % 4
    return row * 8 + col


def take_from(value, x_map=None, dy=0, dz=0, flip=0):
    perm = []
    for x in range(4):
        source_x = x if x_map is None else x_map[x]
        for y in range(4):
            for z in range(4):
                for core in range(2):
                    source = device_index(source_x, y + dy, z + dz, core ^ flip)
                    perm.append((source, device_index(x, y, z, core)))
    return lax.ppermute(value, AXES, perm)


def whole():
    return pl.BlockSpec(memory_space=pltpu.VMEM)


def scalars():
    return pl.BlockSpec(memory_space=pltpu.SMEM)


def params(grid=False):
    return pltpu.CompilerParams(
        vmem_limit_bytes=VMEM_LIMIT, **({"dimension_semantics": ("arbitrary",)} if grid else {})
    )


def unit_kernel(image_ref, image_scale_ref, text_ref, text_scale_ref, out_ref):
    count, width = image_ref.shape
    blocks = image_scale_ref.shape[0]
    size = width // blocks
    for which, (vals, scales_ref) in enumerate(
        ((image_ref, image_scale_ref), (text_ref, text_scale_ref))
    ):
        scales = scales_ref[...].astype(jnp.float32)
        scales = jnp.concatenate([scales] * (count // blocks), axis=0).T
        full = [
            vals[:, k * size : (k + 1) * size].astype(jnp.float32) * scales[:, k : k + 1]
            for k in range(blocks)
        ]
        square = sum(jnp.sum(part * part, axis=-1, keepdims=True) for part in full)
        inv = lax.rsqrt(square + EPS)
        for k in range(blocks):
            out_ref[which * count : (which + 1) * count, k * size : (k + 1) * size] = (
                full[k] * inv
            ).astype(jnp.bfloat16)


def unit_targets(image_vals, image_scales, text_vals, text_scales):
    count, width = image_vals.shape
    return pl.pallas_call(
        unit_kernel,
        out_shape=jax.ShapeDtypeStruct((2 * count, width), jnp.bfloat16),
        in_specs=[whole()] * 4,
        out_specs=whole(),
        compiler_params=params(),
        cost_estimate=pl.CostEstimate(flops=2**20, bytes_accessed=2**20, transcendentals=0),
    )(image_vals, image_scales.T, text_vals, text_scales.T)


def proj_kernel(*refs):
    feature_refs = refs[:8]
    weight_ref, tile_ref, proj_ref, unit_ref = refs[8:]
    step = pl.program_id(0)
    rows = feature_refs[0].shape[0]
    for turn in range(2):

        @pl.when(step == turn)
        def _():
            for k in range(4):
                tile_ref[k * rows : (k + 1) * rows, :] = feature_refs[4 * turn + k][...]

    proj = jnp.dot(tile_ref[...], weight_ref[...], preferred_element_type=jnp.float32)
    inv = lax.rsqrt(jnp.sum(proj * proj, axis=-1, keepdims=True) + EPS)
    proj_ref[...] = proj
    unit_ref[...] = (proj * inv).astype(jnp.bfloat16)


def project(features, weight):
    deep, width = weight.shape
    step = 4 * features[0].shape[0]
    once = pl.Buffered(1)

    def rows_of(array_width):
        return pl.BlockSpec((step, array_width), lambda i: (i, 0))

    return pl.pallas_call(
        proj_kernel,
        grid=(2,),
        out_shape=(
            jax.ShapeDtypeStruct((2 * step, deep), jnp.bfloat16),
            jax.ShapeDtypeStruct((2 * step, width), jnp.float32),
            jax.ShapeDtypeStruct((2 * step, width), jnp.bfloat16),
        ),
        in_specs=[pl.BlockSpec(part.shape, lambda i: (0, 0), pipeline_mode=once) for part in features]
        + [pl.BlockSpec((deep, width), lambda i: (0, 0), pipeline_mode=once)],
        out_specs=(rows_of(deep), rows_of(width), rows_of(width)),
        compiler_params=params(True),
        cost_estimate=pl.CostEstimate(
            flops=4 * step * deep * width, bytes_accessed=12 * 2**20, transcendentals=0
        ),
    )(*features, weight)


def to_column(row):
    parts = []
    for at in range(0, row.shape[1], LANES):
        wide = jnp.broadcast_to(row[:, at : at + LANES], (LANES, LANES))
        parts.append(wide.T)
    return jnp.concatenate(parts, axis=0)


def logits_kernel(count, first, last, *refs):
    refs = list(refs)
    scale_ref, points_ref = refs[:2]
    target_refs = refs[2 : 2 + count]
    refs = refs[2 + count :]
    if not first:
        old_max_ref, old_sum_ref = refs[:2]
        refs = refs[2:]
    logits_ref, col_ref = refs[:2]
    refs = refs[2:]
    if first:
        diag_ref = refs.pop(0)
    if last:
        row_ref = refs.pop(0)
    row_max_ref, row_sum_ref, held_ref, col_max_ref, sem_ref = refs
    rows = points_ref.shape[0]
    chunk = 64
    scale = scale_ref[0] * LOG2E

    def copy_out(j):
        at = slice(j * WIDE, (j + 1) * WIDE)
        return pltpu.make_async_copy(held_ref.at[:, at], logits_ref.at[:, at], sem_ref.at[j])

    for j in range(count):
        at = slice(j * WIDE, (j + 1) * WIDE)
        held_ref[:, at] = scale * lax.dot_general(
            points_ref[...],
            target_refs[j][...],
            (((1,), (1,)), ((), ())),
            preferred_element_type=jnp.float32,
        )
        copy_out(j).start()
        top = None
        for r in range(0, rows, chunk):
            value = held_ref[r : r + chunk, at]
            if j:
                row_max_ref[r : r + chunk, :] = jnp.maximum(row_max_ref[r : r + chunk, :], value)
            elif first:
                row_max_ref[r : r + chunk, :] = value
            else:
                row_max_ref[r : r + chunk, :] = jnp.maximum(old_max_ref[r : r + chunk, :], value)
            part = jnp.max(value.reshape(chunk // 8, 8, WIDE), axis=0)
            top = part if top is None else jnp.maximum(top, part)
        col_max_ref[j : j + 1, :] = jnp.max(top, axis=0, keepdims=True)

    if first:
        rows_at = lax.broadcasted_iota(jnp.int32, (LANES, WIDE), 0)
        cols_at = lax.broadcasted_iota(jnp.int32, (LANES, WIDE), 1) % LANES
        own = jnp.where(rows_at == cols_at, held_ref[:LANES, :WIDE], 0.0)
        diag_ref[...] = jnp.broadcast_to(jnp.sum(own, axis=0, keepdims=True), diag_ref.shape)
        row_sum_ref[...] = jnp.zeros(row_sum_ref.shape, jnp.float32)
    else:
        row_sum_ref[...] = old_sum_ref[...] * jnp.exp2(old_max_ref[...] - row_max_ref[...])

    def sums(j, _):
        at = pl.ds(pl.multiple_of(j * WIDE, WIDE), WIDE)
        top = col_max_ref[pl.ds(j, 1), :]
        total = jnp.zeros((8, WIDE), jnp.float32)
        for r in range(0, rows, chunk):
            value = held_ref[r : r + chunk, at]
            row_sum_ref[r : r + chunk, :] += jnp.exp2(value - row_max_ref[r : r + chunk, :])
            total += jnp.sum(jnp.exp2(value - top).reshape(chunk // 8, 8, WIDE), axis=0)
        col_ref[pl.ds(j, 1), :] = top + jnp.log(jnp.sum(total, axis=0, keepdims=True)) * LOG2E
        return 0

    lax.fori_loop(0, count, sums, 0)
    if last:
        for which in range(2):
            lanes = slice(which * LANES, (which + 1) * LANES)
            for r in range(0, rows, LANES):
                tops = row_max_ref[r : r + LANES, lanes].T
                part = row_sum_ref[r : r + LANES, lanes].T
                top = jnp.max(tops, axis=0, keepdims=True)
                total = jnp.sum(part * jnp.exp2(tops - top), axis=0, keepdims=True)
                row_ref[which : which + 1, r : r + LANES] = top + jnp.log(total) * LOG2E
    for j in range(count):
        copy_out(j).wait()


def logits_of(points, scale, targets, old, last):
    rows = points.shape[0]
    count = len(targets)
    cols = count * WIDE
    first = not old
    lanes = jax.ShapeDtypeStruct((rows, WIDE), jnp.float32)
    held = [pltpu.VMEM(lanes.shape, jnp.float32)] * 2
    outs = [
        jax.ShapeDtypeStruct((rows, cols), jnp.float32),
        jax.ShapeDtypeStruct((count, WIDE), jnp.float32),
    ]
    if first:
        outs.append(jax.ShapeDtypeStruct((8, WIDE), jnp.float32))
    outs += [jax.ShapeDtypeStruct((2, rows), jnp.float32)] if last else [lanes, lanes]
    return pl.pallas_call(
        functools.partial(logits_kernel, count, first, last),
        out_shape=outs,
        in_specs=[scalars()] + [whole()] * (1 + count + len(old)),
        out_specs=[pl.BlockSpec(memory_space=pl.ANY)] + [whole()] * (len(outs) - 1),
        scratch_shapes=(held if last else [])
        + [
            pltpu.VMEM((rows, cols), jnp.float32),
            pltpu.VMEM((count, WIDE), jnp.float32),
            pltpu.SemaphoreType.DMA((count,)),
        ],
        compiler_params=params(),
        cost_estimate=pl.CostEstimate(
            flops=2 * rows * cols * points.shape[1],
            bytes_accessed=4 * rows * cols,
            transcendentals=2 * rows * cols,
        ),
    )(scale, points, *targets, *old)


def grad_kernel(core_ref, scale_ref, *refs):
    logits_refs = refs[:3]
    target_refs = refs[3:19]
    row_ref, col_ref, proj_ref, features_ref, kept_ref, sent_ref = refs[19:25]
    coef_ref, targets_ref, tops_ref, grad_ref, high_ref, low_ref, turned_ref, part_ref = refs[25:33]
    sem_ref = refs[33]
    step = pl.program_id(0)
    size = proj_ref.shape[0]
    scale = scale_ref[0]
    chunk = 64

    def copy_in(k):
        return pltpu.make_async_copy(
            target_refs[k], targets_ref.at[k * WIDE : (k + 1) * WIDE, :], sem_ref.at[k]
        )

    @pl.when(step == 0)
    def _():
        for k in range(16):
            copy_in(k).start()

    tops_ref[...] = jnp.concatenate(
        [to_column(row_ref[which : which + 1, :]) for which in range(2)], axis=1
    )

    def coefs(r, _):
        r_at = pl.ds(pl.multiple_of(r * chunk, chunk), chunk)
        tops = tops_ref[r_at, :]
        k = 0
        for logits_ref in logits_refs:
            for at in range(0, logits_ref.shape[1], WIDE):
                value = logits_ref[r_at, at : at + WIDE]
                coef = jnp.exp2(value - tops) + jnp.exp2(value - col_ref[k : k + 1, :])
                if k == 0:
                    rows_at = lax.broadcasted_iota(jnp.int32, (chunk, WIDE), 0)
                    cols_at = lax.broadcasted_iota(jnp.int32, (chunk, WIDE), 1) % LANES
                    hit = rows_at + (r * chunk + step * size) == cols_at
                    coef = coef - jnp.where(hit, 2.0, 0.0)
                coef_ref[r_at, k * WIDE : (k + 1) * WIDE] = coef.astype(jnp.bfloat16)
                k += 1
        return 0

    lax.fori_loop(0, size // chunk, coefs, 0)
    rows = pl.ds(pl.multiple_of(step * size, size), size)
    turned_ref[:, rows] = features_ref[...].T

    @pl.when(step == 0)
    def _():
        for k in range(16):
            copy_in(k).wait()

    def columns(n, _):
        at = pl.ds(pl.multiple_of(n * WIDE, WIDE), WIDE)
        grad_ref[:, at] = jnp.dot(
            coef_ref[...], targets_ref[:, at], preferred_element_type=jnp.float32
        )
        return 0

    lax.fori_loop(0, proj_ref.shape[1] // WIDE, columns, 0)

    def finish(r, _):
        r_at = pl.ds(pl.multiple_of(r * chunk, chunk), chunk)
        grad = grad_ref[r_at, :] * (scale * 0.25)
        proj = proj_ref[r_at, :]
        inv = lax.rsqrt(jnp.sum(proj * proj, axis=-1, keepdims=True) + EPS)
        along = jnp.sum(proj * grad, axis=-1, keepdims=True)
        grad = inv * (grad - along * inv * inv * proj)
        high = grad.astype(jnp.bfloat16)
        at = pl.ds(pl.multiple_of(step * size + r * chunk, chunk), chunk)
        high_ref[at, :] = high
        low_ref[at, :] = (grad - high.astype(jnp.float32)).astype(jnp.bfloat16)
        return 0

    lax.fori_loop(0, size // chunk, finish, 0, unroll=2)

    @pl.when(step == pl.num_programs(0) - 1)
    def _():
        core = core_ref[0]
        deep = turned_ref.shape[0]
        cut = deep // 16

        def products(n, _):
            at = pl.ds(pl.multiple_of(n * WIDE, WIDE), WIDE)
            part_ref[...] = jnp.dot(
                turned_ref[...], high_ref[:, at], preferred_element_type=jnp.float32
            ) + jnp.dot(turned_ref[...], low_ref[:, at], preferred_element_type=jnp.float32)
            for v in range(8):
                for side in range(2):
                    lanes = slice(side * LANES, (side + 1) * LANES)
                    for out_ref, half in ((kept_ref, core), (sent_ref, 1 - core)):
                        from_row = pl.multiple_of(half * (deep // 2) + v * cut, 8)
                        out_ref[v * 8 + 2 * n + side] = part_ref[pl.ds(from_row, cut), lanes]
            return 0

        lax.fori_loop(0, high_ref.shape[1] // WIDE, products, 0)


def grad_of(core, scale, logits, targets, row_lse, col_lse, proj, features):
    rows, width = proj.shape
    deep = features.shape[1]
    step = 512
    cut = deep // 16
    once = pl.Buffered(1)
    piece = jax.ShapeDtypeStruct((64, cut, LANES), jnp.float32)
    piece_spec = pl.BlockSpec(piece.shape, lambda i: (0, 0, 0), pipeline_mode=once)
    cols = sum(part.shape[1] for part in logits)
    return pl.pallas_call(
        grad_kernel,
        grid=(rows // step,),
        out_shape=(piece, piece),
        in_specs=[scalars(), scalars()]
        + [pl.BlockSpec((step, part.shape[1]), lambda i: (i, 0)) for part in logits]
        + [pl.BlockSpec(memory_space=pl.ANY)] * len(targets)
        + [
            pl.BlockSpec((2, step), lambda i: (0, i)),
            pl.BlockSpec(col_lse.shape, lambda i: (0, 0), pipeline_mode=once),
            pl.BlockSpec((step, width), lambda i: (i, 0)),
            pl.BlockSpec((step, deep), lambda i: (i, 0)),
        ],
        out_specs=(piece_spec, piece_spec),
        scratch_shapes=[
            pltpu.VMEM((step, cols), jnp.bfloat16),
            pltpu.VMEM((cols, width), jnp.bfloat16),
            pltpu.VMEM((step, WIDE), jnp.float32),
            pltpu.VMEM((step, width), jnp.float32),
            pltpu.VMEM((rows, width), jnp.bfloat16),
            pltpu.VMEM((rows, width), jnp.bfloat16),
            pltpu.VMEM((deep, rows), jnp.bfloat16),
            pltpu.VMEM((deep, WIDE), jnp.float32),
            pltpu.SemaphoreType.DMA((len(targets),)),
        ],
        compiler_params=params(True),
        cost_estimate=pl.CostEstimate(
            flops=2 * rows * cols * width, bytes_accessed=32 * 2**20, transcendentals=2 * rows * cols
        ),
    )(core, scale, *logits, *targets, row_lse, col_lse, proj, features)


def assemble_kernel(core_ref, here_ref, there_ref, out_ref, loss_ref):
    step = pl.program_id(0)
    cut = out_ref.shape[0]

    @pl.when(step == 0)
    def _():
        loss_ref[...] = jnp.zeros(loss_ref.shape, jnp.float32)

    def fill(ref):
        for w in range(8):
            value = ref[w]
            flags = [value[cut + k : cut + k + 1, :] for k in range(4)]
            out_ref[:, w * LANES : (w + 1) * LANES] = value[:cut] * jnp.exp2(-flags[0])
            loss_ref[...] += flags[1] * 16.0 + flags[2] / 64.0 + flags[3] / 16384.0

    @pl.when(step < 8)
    def _():
        fill(here_ref)

    @pl.when(step >= 8)
    def _():
        fill(there_ref)


def assemble(core, here, there, cut):
    deep, lanes = here.shape[1:]
    return pl.pallas_call(
        assemble_kernel,
        grid_spec=pltpu.PrefetchScalarGridSpec(
            num_scalar_prefetch=1,
            grid=(16,),
            in_specs=[
                pl.BlockSpec((8, deep, lanes), lambda i, core: (jnp.minimum(i, 7), 0, 0)),
                pl.BlockSpec((8, deep, lanes), lambda i, core: (jnp.maximum(i - 8, 0), 0, 0)),
            ],
            out_specs=(
                pl.BlockSpec((cut, 8 * lanes), lambda i, core: (i ^ (core[0] * 8), 0)),
                pl.BlockSpec((8, lanes), lambda i, core: (0, 0)),
            ),
        ),
        out_shape=(
            jax.ShapeDtypeStruct((16 * cut, 8 * lanes), jnp.float32),
            jax.ShapeDtypeStruct((8, lanes), jnp.float32),
        ),
        compiler_params=params(True),
        cost_estimate=pl.CostEstimate(flops=2**20, bytes_accessed=9 * 2**20, transcendentals=0),
    )(core, here, there)


def point_group(x, y, z, core):
    return (x // 2, y, core), (x % 2, z)


def target_group(x, y, z, core):
    pair = 0 if x in (0, 3) else 1
    return (pair, z), (core, 1 if x >= 2 else 0, y)


def same_core_group(x, y, z, core):
    return (core,), (x, y, z)


def groups_of(rule):
    found = {}
    for x in range(4):
        for y in range(4):
            for z in range(4):
                for core in range(2):
                    group, place = rule(x, y, z, core)
                    found.setdefault(group, []).append((place, device_index(x, y, z, core)))
    return [[device for _, device in sorted(found[group])] for group in sorted(found)]


def swap_blocks(value, rule):
    return lax.all_to_all(
        value, AXES, split_axis=0, concat_axis=0, axis_index_groups=groups_of(rule), tiled=True
    )


def rolled(value, shift, axis):
    out = value
    for step in range(1, 4):
        out = jnp.where(shift == step, jnp.roll(value, step, axis=axis), out)
    return out


def flipped(value, flag, axis):
    return jnp.where(flag == 1, jnp.flip(value, axis), value)


def merged(stack):
    top = jnp.max(stack, axis=0)
    return top + jnp.log(jnp.sum(jnp.exp2(stack - top), axis=0)) * LOG2E


def row_exchange(local):
    shape = (2, 2, 4, local.shape[1] // 8)

    def add(value, got):
        return merged(jnp.stack([value, got.reshape(local.shape)]))

    got = take_from(local, x_map=X_POINT).reshape(shape)
    value = add(local, got[:, ::-1])
    for step in (1, 2):
        got = take_from(value, dz=step).reshape(shape)
        value = add(value, jnp.roll(got, step, axis=2))
    return value


def col_exchange(local, core, flip, y):
    wide = local.shape[1]
    placed = jnp.stack(
        [
            local[ORDER.index((c, a, d))]
            for c in range(2)
            for a in range(2)
            for d in range(4)
        ]
    ).reshape(2, 2, 4, wide)
    placed = rolled(flipped(flipped(placed, core, 0), flip, 1), y, 2).reshape(16, wide)
    parts = swap_blocks(jnp.broadcast_to(placed, (16, 16, wide)), target_group)
    total = merged(parts).reshape(2, 2, 4, wide)
    total = flipped(flipped(rolled(total, (4 - y) % 4, 2), flip, 1), core, 0)
    return jnp.stack([total[place] for place in ORDER])


def gather_points(own):
    def near(value):
        return take_from(value, x_map=X_POINT)

    beside, after, before = near(own), take_from(own, dz=1), take_from(own, dz=-1)
    beside_before, far, beside_after = take_from(beside, dz=-1), take_from(after, dz=1), near(after)
    beside_far = take_from(beside_after, dz=1)
    return [own, after, far, before, beside, beside_after, beside_far, beside_before]


def gather_targets(own):
    def near(value):
        return take_from(value, x_map=X_TARGET)

    def with_other(blocks):
        return blocks + [take_from(block, flip=1) for block in blocks]

    beside, after, before = near(own), take_from(own, dy=1), take_from(own, dy=-1)
    first = with_other([own, beside, after, before])
    beside_before, far, beside_after = take_from(beside, dy=-1), take_from(after, dy=1), near(after)
    second = with_other([beside_before, far, beside_after])
    third = with_other([take_from(beside_after, dy=1)])
    return [first, second, third]


def total_sum(kept, sent, local_loss, core):
    count, cut, lanes = kept.shape
    half = kept + take_from(sent, flip=1)
    own = jnp.sum(swap_blocks(half, same_core_group), axis=0)
    power = 14.0 - jnp.floor(jnp.log2(jnp.maximum(jnp.max(jnp.abs(own)), 1e-30)))
    small = (own * jnp.exp2(power)).astype(jnp.float16)
    first = (local_loss / 16.0).astype(jnp.float16)
    rest = local_loss - first.astype(jnp.float32) * 16.0
    second = (rest * 64.0).astype(jnp.float16)
    rest = rest - second.astype(jnp.float32) / 64.0
    third = (rest * 16384.0).astype(jnp.float16)
    values = [power.astype(jnp.float16), first, second, third]
    tail = jnp.stack([values[min(i, 3)] for i in range(8)])
    tail = jnp.broadcast_to(tail[:, None], (8, lanes))
    small = jnp.concatenate([small, tail], axis=0)
    here = swap_blocks(jnp.broadcast_to(small, (count,) + small.shape), same_core_group)
    there = take_from(here, flip=1)
    grad_w, loss = assemble(core, here.astype(jnp.float32), there.astype(jnp.float32), cut)
    return grad_w, loss[0, 0]


def body(features, proj_weight, image_vals, image_scales, text_vals, text_scales, logit_scale):
    rows = features.shape[0]
    total = rows * lax.axis_size("row") * lax.axis_size("col")
    row_index = lax.axis_index("row")
    col_index = lax.axis_index("col")
    x = (col_index // 4) * 2 + row_index // 8
    y = (row_index // 2) % 4
    core = row_index % 2

    own = unit_targets(image_vals, image_scales, text_vals, text_scales)
    targets = gather_targets(own)
    tile, proj, points = project(gather_points(features), proj_weight)
    logits, cols, old = [], [], []
    for n, blocks in enumerate(targets):
        out = logits_of(points, logit_scale, blocks, old, n == 2)
        logits.append(out[0])
        cols.append(out[1])
        if n == 0:
            diag = out[2]
        old = out[-2:]
    col_lse = col_exchange(jnp.concatenate(cols, axis=0), core, x // 2, y)
    row_lse = row_exchange(old[-1])
    local_loss = jnp.sum(row_lse[:, :rows]) + jnp.sum(col_lse[0]) - 2.0 * jnp.sum(diag[0])
    core = core.astype(jnp.int32).reshape(1)
    kept, sent = grad_of(
        core, logit_scale, logits, sum(targets, []), row_lse, col_lse, proj, tile
    )
    grad_w, loss = total_sum(kept, sent, local_loss * LN2, core)
    return (loss / (4.0 * total), grad_w)


def solution(mesh):
    return jax.shard_map(
        body,
        mesh=mesh,
        in_specs=(
            P(("row", "col"), None),
            P(),
            P(("row", "col"), None),
            P(("row", "col"), None),
            P(("row", "col"), None),
            P(("row", "col"), None),
            P(),
        ),
        out_specs=(P(), P()),
        check_vma=False,
    )
```

```python
import functools
import jax
import jax.numpy as jnp
from jax import lax
from jax.experimental import pallas as pl
from jax.experimental.pallas import tpu as pltpu
from jax.sharding import PartitionSpec as P

EPS = 1e-06
LOG2E = 1.4426950408889634
LN2 = 0.6931471805599453
SAFE = 60.0
AXES = ("row", "col")
X_POINT = (1, 0, 3, 2)
X_TARGET = (3, 2, 1, 0)
LANES = 128
WIDE = 2 * LANES
BATCHES = (((0, 0), (1, 0), (0, 1), (0, 3)), ((1, 3), (0, 2), (1, 1), (1, 2)))
ORDER = [(core,) + place for batch in BATCHES for core in range(2) for place in batch]
POINT_ORDER = (0, 1, 3, 4, 2, 5, 7, 6)


def device_index(x, y, z, core):
    row = ((x % 2) * 4 + y % 4) * 2 + core
    col = (x // 2) * 4 + z % 4
    return row * 8 + col


def take_from(value, x_map=None, dy=0, dz=0, flip=0):
    perm = []
    for x in range(4):
        source_x = x if x_map is None else x_map[x]
        for y in range(4):
            for z in range(4):
                for core in range(2):
                    source = device_index(source_x, y + dy, z + dz, core ^ flip)
                    perm.append((source, device_index(x, y, z, core)))
    return lax.ppermute(value, AXES, perm)


def whole():
    return pl.BlockSpec(memory_space=pltpu.VMEM)


def scalars():
    return pl.BlockSpec(memory_space=pltpu.SMEM)


def anywhere():
    return pl.BlockSpec(memory_space=pl.ANY)


def params(mib, grid=False):
    return pltpu.CompilerParams(
        vmem_limit_bytes=mib * 2**20, **({"dimension_semantics": ("arbitrary",)} if grid else {})
    )


def canonical(block):
    core, flip, step = block
    return (core * 2 + flip) * 4 + step


def unit_kernel(image_ref, image_scale_ref, text_ref, text_scale_ref, out_ref):
    count, width = image_ref.shape
    blocks = image_scale_ref.shape[0]
    size = width // blocks
    for which, (vals, scales_ref) in enumerate(
        ((image_ref, image_scale_ref), (text_ref, text_scale_ref))
    ):
        scales = scales_ref[...].astype(jnp.float32)
        scales = jnp.concatenate([scales] * (count // blocks), axis=0).T
        full = [
            vals[:, k * size : (k + 1) * size].astype(jnp.float32) * scales[:, k : k + 1]
            for k in range(blocks)
        ]
        square = sum(jnp.sum(part * part, axis=-1, keepdims=True) for part in full)
        inv = lax.rsqrt(square + EPS)
        for k in range(blocks):
            out_ref[which * count : (which + 1) * count, k * size : (k + 1) * size] = (
                full[k] * inv
            ).astype(jnp.bfloat16)


def unit_targets(image_vals, image_scales, text_vals, text_scales):
    count, width = image_vals.shape
    return pl.pallas_call(
        unit_kernel,
        out_shape=jax.ShapeDtypeStruct((2 * count, width), jnp.bfloat16),
        in_specs=[whole()] * 4,
        out_specs=whole(),
        compiler_params=params(16),
        cost_estimate=pl.CostEstimate(flops=2**20, bytes_accessed=2**20, transcendentals=0),
    )(image_vals, image_scales.T, text_vals, text_scales.T)


def proj_kernel(*refs):
    feature_refs = refs[:4]
    weight_ref = refs[4]
    outs, (tile_ref, weight_in_ref, proj_ref, unit_ref, in_sem, out_sem) = refs[-9:-6], refs[-6:]
    base = 0 if len(refs) == 14 else tile_ref.shape[0]
    rows = feature_refs[0].shape[0]
    step = 2 * rows
    incoming = [pltpu.make_async_copy(weight_ref, weight_in_ref, in_sem.at[4])]
    for k in range(4):
        to = tile_ref.at[k * rows : (k + 1) * rows, :]
        incoming.append(pltpu.make_async_copy(feature_refs[k], to, in_sem.at[k]))
    for copy in incoming:
        copy.start()
    for copy in incoming:
        copy.wait()
    outgoing = []

    def send(held_ref, out_ref, at, count):
        copy = pltpu.make_async_copy(
            held_ref.at[at : at + count, :],
            out_ref.at[base + at : base + at + count, :],
            out_sem.at[len(outgoing)],
        )
        copy.start()
        outgoing.append(copy)

    send(tile_ref, outs[0], 0, 2 * step)
    for at in range(0, 2 * step, step):
        proj = jnp.dot(
            tile_ref[at : at + step, :], weight_in_ref[...], preferred_element_type=jnp.float32
        )
        inv = lax.rsqrt(jnp.sum(proj * proj, axis=-1, keepdims=True) + EPS)
        proj_ref[at : at + step, :] = proj
        unit_ref[at : at + step, :] = (proj * inv).astype(jnp.bfloat16)
        send(proj_ref, outs[1], at, step)
        send(unit_ref, outs[2], at, step)
    for copy in outgoing:
        copy.wait()


def project(features, weight, done):
    deep, width = weight.shape
    rows = 4 * features[0].shape[0]
    return pl.pallas_call(
        proj_kernel,
        out_shape=(
            jax.ShapeDtypeStruct((2 * rows, deep), jnp.bfloat16),
            jax.ShapeDtypeStruct((2 * rows, width), jnp.float32),
            jax.ShapeDtypeStruct((2 * rows, width), jnp.bfloat16),
        ),
        in_specs=[anywhere()] * (5 + len(done)),
        out_specs=(anywhere(), anywhere(), anywhere()),
        input_output_aliases={5 + k: k for k in range(len(done))},
        scratch_shapes=[
            pltpu.VMEM((rows, deep), jnp.bfloat16),
            pltpu.VMEM((deep, width), jnp.bfloat16),
            pltpu.VMEM((rows, width), jnp.float32),
            pltpu.VMEM((rows, width), jnp.bfloat16),
            pltpu.SemaphoreType.DMA((5,)),
            pltpu.SemaphoreType.DMA((5,)),
        ],
        compiler_params=params(32),
        cost_estimate=pl.CostEstimate(
            flops=2 * rows * deep * width, bytes_accessed=6 * 2**20, transcendentals=0
        ),
    )(*features, weight, *done)


def to_column(row):
    parts = []
    for at in range(0, row.shape[1], LANES):
        wide = jnp.broadcast_to(row[:, at : at + LANES], (LANES, LANES))
        parts.append(wide.T)
    return jnp.concatenate(parts, axis=0)


def logits_kernel(last, *refs):
    refs = list(refs)
    scale_ref, points_any = refs[:2]
    target_refs = refs[2:10]
    count = len(target_refs)
    if last:
        old_max_any, old_sum_any, old_col_ref, logits_ref, row_ref, all_col_ref = refs[10:16]
        row_max_ref, row_sum_ref, col_ref = refs[16:19]
        old_max_ref, old_sum_ref = refs[19:21]
        olds = ((old_max_any, old_max_ref), (old_sum_any, old_sum_ref))
    else:
        logits_ref, col_ref, diag_ref, row_max_ref, row_sum_ref = refs[10:15]
        olds = ()
    points_ref, targets_ref, held_ref, col_max_ref, weight_ref, out_sem, in_sem = refs[-7:]
    rows = points_ref.shape[0]
    chunk = 64
    scale = scale_ref[0] * LOG2E

    incoming = [pltpu.make_async_copy(points_any, points_ref, in_sem.at[count])]
    for j in range(count):
        to = targets_ref.at[j * WIDE : (j + 1) * WIDE, :]
        incoming.append(pltpu.make_async_copy(target_refs[j], to, in_sem.at[j]))
    for k, (source, to) in enumerate(olds):
        incoming.append(pltpu.make_async_copy(source, to, in_sem.at[count + 1 + k]))
    for copy in incoming:
        copy.start()
    incoming[0].wait()
    for copy in incoming[count + 1 :]:
        copy.wait()

    def copy_out(j):
        at = slice(j * WIDE, (j + 1) * WIDE)
        return pltpu.make_async_copy(held_ref.at[:, at], logits_ref.at[:, at], out_sem.at[j])

    for j in range(count):
        at = slice(j * WIDE, (j + 1) * WIDE)
        incoming[1 + j].wait()
        held_ref[:, at] = scale * lax.dot_general(
            points_ref[...],
            targets_ref[at, :],
            (((1,), (1,)), ((), ())),
            preferred_element_type=jnp.float32,
        )
        copy_out(j).start()
        top = None
        for r in range(0, rows, chunk):
            r_at = slice(r, r + chunk)
            value = held_ref[r_at, at]
            if j:
                row_max_ref[r_at, :] = jnp.maximum(row_max_ref[r_at, :], value)
            elif last:
                row_max_ref[r_at, :] = jnp.maximum(old_max_ref[r_at, :], value)
            else:
                row_max_ref[r_at, :] = value
            part = jnp.max(value.reshape(chunk // 8, 8, WIDE), axis=0)
            top = part if top is None else jnp.maximum(top, part)
        col_max_ref[j : j + 1, :] = jnp.max(top, axis=0, keepdims=True)

    peak = jnp.max(row_max_ref[...], axis=0, keepdims=True)
    near = jnp.min(col_max_ref[...] - peak) > -SAFE
    for r in range(0, rows, chunk):
        r_at = slice(r, r + chunk)
        weight_ref[r_at, :] = jnp.exp2(row_max_ref[r_at, :] - peak)
        if last:
            shrink = jnp.exp2(old_max_ref[r_at, :] - row_max_ref[r_at, :])
            row_sum_ref[r_at, :] = old_sum_ref[r_at, :] * shrink
        else:
            row_sum_ref[r_at, :] = jnp.zeros((chunk, WIDE), jnp.float32)

    def finish(j, top, total):
        total = jnp.sum(total, axis=0, keepdims=True)
        col_ref[pl.ds(j, 1), :] = top + jnp.log(total) * LOG2E

    def near_sums(j, _):
        at = pl.ds(pl.multiple_of(j * WIDE, WIDE), WIDE)
        total = jnp.zeros((8, WIDE), jnp.float32)
        for r in range(0, rows, chunk):
            r_at = slice(r, r + chunk)
            part = jnp.exp2(held_ref[r_at, at] - row_max_ref[r_at, :])
            row_sum_ref[r_at, :] += part
            total += jnp.sum((part * weight_ref[r_at, :]).reshape(chunk // 8, 8, WIDE), axis=0)
        finish(j, peak, total)
        return 0

    def far_sums(j, _):
        at = pl.ds(pl.multiple_of(j * WIDE, WIDE), WIDE)
        top = col_max_ref[pl.ds(j, 1), :]
        total = jnp.zeros((8, WIDE), jnp.float32)
        for r in range(0, rows, chunk):
            r_at = slice(r, r + chunk)
            value = held_ref[r_at, at]
            row_sum_ref[r_at, :] += jnp.exp2(value - row_max_ref[r_at, :])
            total += jnp.sum(jnp.exp2(value - top).reshape(chunk // 8, 8, WIDE), axis=0)
        finish(j, top, total)
        return 0

    @pl.when(near)
    def _():
        lax.fori_loop(0, count, near_sums, 0)

    @pl.when(jnp.logical_not(near))
    def _():
        lax.fori_loop(0, count, far_sums, 0)

    if last:
        for k, block in enumerate(ORDER):
            source = old_col_ref if k < count else col_ref
            at, to = k % count, canonical(block)
            all_col_ref[to : to + 1, :] = source[at : at + 1, :]
        for which in range(2):
            lanes = slice(which * LANES, (which + 1) * LANES)
            for k, place in enumerate(POINT_ORDER):
                r_at = slice(k * LANES, (k + 1) * LANES)
                tops = row_max_ref[r_at, lanes].T
                part = row_sum_ref[r_at, lanes].T
                top = jnp.max(tops, axis=0, keepdims=True)
                total = jnp.sum(part * jnp.exp2(tops - top), axis=0, keepdims=True)
                row_ref[which : which + 1, place * LANES : (place + 1) * LANES] = (
                    top + jnp.log(total) * LOG2E
                )
    else:
        rows_at = lax.broadcasted_iota(jnp.int32, (LANES, WIDE), 0)
        cols_at = lax.broadcasted_iota(jnp.int32, (LANES, WIDE), 1) % LANES
        own = jnp.where(rows_at == cols_at, held_ref[:LANES, :WIDE], 0.0)
        diag_ref[...] = jnp.broadcast_to(jnp.sum(own, axis=0, keepdims=True), diag_ref.shape)
    for j in range(count):
        copy_out(j).wait()


def logits_of(points, scale, targets, old):
    rows, width = points.shape
    count = len(targets)
    cols = count * WIDE
    last = bool(old)
    lanes = (rows, WIDE)
    if last:
        shapes = [(2, rows), (2 * count, WIDE)]
        held = [lanes, lanes, (count, WIDE), lanes, lanes]
        old_specs = [anywhere(), anywhere(), whole()]
    else:
        shapes = [(count, WIDE), (8, WIDE), lanes, lanes]
        held = []
        old_specs = []
    return pl.pallas_call(
        functools.partial(logits_kernel, last),
        out_shape=[jax.ShapeDtypeStruct(shape, jnp.float32) for shape in [(rows, cols)] + shapes],
        in_specs=[scalars()] + [anywhere()] * (1 + count) + old_specs,
        out_specs=[anywhere()] + [whole()] * len(shapes),
        scratch_shapes=[pltpu.VMEM(shape, jnp.float32) for shape in held]
        + [
            pltpu.VMEM((rows, width), jnp.bfloat16),
            pltpu.VMEM((cols, width), jnp.bfloat16),
            pltpu.VMEM((rows, cols), jnp.float32),
            pltpu.VMEM((count, WIDE), jnp.float32),
            pltpu.VMEM(lanes, jnp.float32),
            pltpu.SemaphoreType.DMA((count,)),
            pltpu.SemaphoreType.DMA((count + 3,)),
        ],
        compiler_params=params(40),
        cost_estimate=pl.CostEstimate(
            flops=2 * rows * cols * points.shape[1],
            bytes_accessed=4 * rows * cols,
            transcendentals=rows * cols,
        ),
    )(scale, points, *targets, *old)


def grad_kernel(place_ref, scale_ref, *refs):
    logits_refs = refs[:2]
    target_refs = refs[2:18]
    row_ref, all_col_ref, diag_ref, proj_ref, turned_any, kept_ref, sent_ref, loss_ref = refs[18:26]
    coef_ref, targets_ref, tops_ref, shares_ref, edges_ref, high_ref, low_ref = refs[26:33]
    part_ref, turned_ref, sem_ref = refs[33:]
    step = pl.program_id(0)
    size = proj_ref.shape[0]
    scale = scale_ref[0]
    chunk = 64

    def copy_in(k):
        if k == 16:
            return pltpu.make_async_copy(turned_any, turned_ref, sem_ref.at[k])
        return pltpu.make_async_copy(
            target_refs[k], targets_ref.at[k * WIDE : (k + 1) * WIDE, :], sem_ref.at[k]
        )

    peak = jnp.max(row_ref[...])
    near = peak - jnp.min(all_col_ref[...]) < SAFE

    @pl.when(step == 0)
    def _():
        for k in range(17):
            copy_in(k).start()
        for k, block in enumerate(ORDER):
            at = canonical(block)
            edges_ref[k : k + 1, :] = all_col_ref[at : at + 1, :]
        for k, place in enumerate(POINT_ORDER):
            for which in range(2):
                row = row_ref[which : which + 1, place * LANES : (place + 1) * LANES]
                r_at = slice(k * LANES, (k + 1) * LANES)
                lanes = slice(which * LANES, (which + 1) * LANES)
                tops_ref[r_at, lanes] = to_column(row)
                shares_ref[r_at, lanes] = to_column(jnp.exp2(row - peak))
        both = edges_ref[:1, :] - 2.0 * diag_ref[:1, :]
        both = both[:, :LANES] + both[:, LANES:] + row_ref[:1, :LANES] + row_ref[1:2, :LANES]
        loss_ref[...] = jnp.broadcast_to(both, loss_ref.shape)

    def own_hits(r):
        rows_at = lax.broadcasted_iota(jnp.int32, (chunk, WIDE), 0) + r + step * size
        cols_at = lax.broadcasted_iota(jnp.int32, (chunk, WIDE), 1) % LANES
        return jnp.where(rows_at == cols_at, 2.0, 0.0)

    def coefs(is_near):
        k = 0
        for logits_ref in logits_refs:
            for at in range(0, logits_ref.shape[1], WIDE):
                edge = edges_ref[k : k + 1, :]
                rise = jnp.exp2(peak - edge)
                for r in range(0, size, chunk):
                    value = logits_ref[r : r + chunk, at : at + WIDE]
                    r_at = pl.ds(pl.multiple_of(step * size + r, chunk), chunk)
                    coef = jnp.exp2(value - tops_ref[r_at, :])
                    if is_near:
                        coef = coef + coef * (shares_ref[r_at, :] * rise)
                    else:
                        coef = coef + jnp.exp2(value - edge)
                    if k == 0 and r < LANES:
                        coef = coef - own_hits(r)
                    coef_ref[r : r + chunk, k * WIDE : (k + 1) * WIDE] = coef.astype(jnp.bfloat16)
                k += 1

    @pl.when(near)
    def _():
        coefs(True)

    @pl.when(jnp.logical_not(near))
    def _():
        coefs(False)

    @pl.when(step == 0)
    def _():
        for k in range(16):
            copy_in(k).wait()

    grad = jnp.dot(coef_ref[...], targets_ref[...], preferred_element_type=jnp.float32)
    grad = grad * (scale * 0.25)
    proj = proj_ref[...]
    inv = lax.rsqrt(jnp.sum(proj * proj, axis=-1, keepdims=True) + EPS)
    along = jnp.sum(proj * grad, axis=-1, keepdims=True)
    grad = inv * (grad - along * inv * inv * proj)
    high = grad.astype(jnp.bfloat16)
    rows = pl.ds(pl.multiple_of(step * size, size), size)
    high_ref[rows, :] = high
    low_ref[rows, :] = (grad - high.astype(jnp.float32)).astype(jnp.bfloat16)

    @pl.when(step == pl.num_programs(0) - 1)
    def _():
        copy_in(16).wait()
        core = place_ref[0]
        deep = turned_ref.shape[0]
        cut = deep // 16

        def products(n, _):
            at = pl.ds(pl.multiple_of(n * WIDE, WIDE), WIDE)
            part_ref[...] = jnp.dot(
                turned_ref[...], high_ref[:, at], preferred_element_type=jnp.float32
            ) + jnp.dot(turned_ref[...], low_ref[:, at], preferred_element_type=jnp.float32)
            for v in range(8):
                for side in range(2):
                    lanes = slice(side * LANES, (side + 1) * LANES)
                    for out_ref, half in ((kept_ref, core), (sent_ref, 1 - core)):
                        from_row = pl.multiple_of(half * (deep // 2) + v * cut, 8)
                        out_ref[v * 8 + 2 * n + side] = part_ref[pl.ds(from_row, cut), lanes]
            return 0

        lax.fori_loop(0, high_ref.shape[1] // WIDE, products, 0)


def grad_of(place, scale, logits, targets, row_lse, col_lse, diag, proj, turned):
    rows, width = proj.shape
    deep = turned.shape[0]
    step = 256
    cut = deep // 16
    piece = jax.ShapeDtypeStruct((64, cut, LANES), jnp.float32)
    cols = sum(part.shape[1] for part in logits)
    return pl.pallas_call(
        grad_kernel,
        grid=(rows // step,),
        out_shape=(piece, piece, jax.ShapeDtypeStruct((8, LANES), jnp.float32)),
        in_specs=[scalars(), scalars()]
        + [pl.BlockSpec((step, part.shape[1]), lambda i: (i, 0)) for part in logits]
        + [anywhere()] * len(targets)
        + [whole(), whole(), whole()]
        + [pl.BlockSpec((step, width), lambda i: (i, 0)), anywhere()],
        out_specs=(whole(), whole(), whole()),
        scratch_shapes=[
            pltpu.VMEM((step, cols), jnp.bfloat16),
            pltpu.VMEM((cols, width), jnp.bfloat16),
            pltpu.VMEM((rows, WIDE), jnp.float32),
            pltpu.VMEM((rows, WIDE), jnp.float32),
            pltpu.VMEM((16, WIDE), jnp.float32),
            pltpu.VMEM((rows, width), jnp.bfloat16),
            pltpu.VMEM((rows, width), jnp.bfloat16),
            pltpu.VMEM((deep, WIDE), jnp.float32),
            pltpu.VMEM((deep, rows), jnp.bfloat16),
            pltpu.SemaphoreType.DMA((len(targets) + 1,)),
        ],
        compiler_params=params(44, True),
        cost_estimate=pl.CostEstimate(
            flops=2 * rows * cols * width, bytes_accessed=32 * 2**20, transcendentals=rows * cols
        ),
    )(place, scale, *logits, *targets, row_lse, col_lse, diag, proj, turned)


def assemble_kernel(place_ref, here_ref, there_ref, out_ref, loss_ref, held_ref, sem_ref):
    cut = here_ref.shape[1] - 8
    half = 8 * cut
    copies = []
    loss = jnp.zeros((1, LANES), jnp.float32)
    for turn, ref in enumerate((here_ref, there_ref)):
        from_row = pl.multiple_of((place_ref[0] ^ turn) * half, 8)
        for v in range(8):
            for w in range(8):
                flags = [ref[v * 8 + w, cut + k : cut + k + 1, :] for k in range(4)]
                held_ref[turn, v * cut : (v + 1) * cut, w * LANES : (w + 1) * LANES] = ref[
                    v * 8 + w, :cut
                ] * jnp.exp2(-flags[0])
                loss += flags[1] * 16.0 + flags[2] / 64.0 + flags[3] / 16384.0
        copy = pltpu.make_async_copy(
            held_ref.at[turn], out_ref.at[pl.ds(from_row, half), :], sem_ref.at[turn]
        )
        copy.start()
        copies.append(copy)
    loss_ref[...] = jnp.broadcast_to(loss, loss_ref.shape)
    for copy in copies:
        copy.wait()


def assemble(place, here, there):
    cut = here.shape[1] - 8
    return pl.pallas_call(
        assemble_kernel,
        in_specs=[scalars(), whole(), whole()],
        out_specs=(anywhere(), whole()),
        out_shape=(
            jax.ShapeDtypeStruct((16 * cut, 8 * LANES), jnp.float32),
            jax.ShapeDtypeStruct((8, LANES), jnp.float32),
        ),
        scratch_shapes=[
            pltpu.VMEM((2, 8 * cut, 8 * LANES), jnp.float32),
            pltpu.SemaphoreType.DMA((2,)),
        ],
        compiler_params=params(16),
        cost_estimate=pl.CostEstimate(flops=2**20, bytes_accessed=9 * 2**20, transcendentals=0),
    )(place, here, there)


def same_core_group(x, y, z, core):
    return (core,), (x, y, z)


def groups_of(rule):
    found = {}
    for x in range(4):
        for y in range(4):
            for z in range(4):
                for core in range(2):
                    group, place = rule(x, y, z, core)
                    found.setdefault(group, []).append((place, device_index(x, y, z, core)))
    return [[device for _, device in sorted(found[group])] for group in sorted(found)]


def swap_blocks(value, rule):
    return lax.all_to_all(
        value, AXES, split_axis=0, concat_axis=0, axis_index_groups=groups_of(rule), tiled=True
    )


def merged(value, got):
    low, high = jnp.minimum(value, got), jnp.maximum(value, got)
    return high + jnp.log(1.0 + jnp.exp2(low - high)) * LOG2E


def exchange_statistics(rows, cols):
    row_shape = (2, 2, 4, rows.shape[1] // 8)
    col_shape = (2, 2, 4, cols.shape[1])

    def row_add(value, got):
        return merged(value, got.reshape(rows.shape))

    def col_add(value, got):
        return merged(value, got.reshape(cols.shape))

    got_rows = take_from(rows, x_map=X_POINT)
    got_cols = take_from(cols, flip=1)
    rows = row_add(rows, got_rows.reshape(row_shape)[:, ::-1])
    cols = col_add(cols, got_cols.reshape(col_shape)[::-1])
    got_rows = take_from(rows, dz=1)
    got_cols = take_from(cols, x_map=X_TARGET)
    rows = row_add(rows, jnp.roll(got_rows.reshape(row_shape), 1, axis=2))
    cols = col_add(cols, got_cols.reshape(col_shape)[:, ::-1])
    got_rows = take_from(rows, dz=2)
    got_cols = take_from(cols, dy=1)
    rows = row_add(rows, jnp.roll(got_rows.reshape(row_shape), 2, axis=2))
    cols = col_add(cols, jnp.roll(got_cols.reshape(col_shape), 1, axis=2))
    got_cols = take_from(cols, dy=2)
    return rows, col_add(cols, jnp.roll(got_cols.reshape(col_shape), 2, axis=2))


def gather_and_project(own_points, own_targets, weight):
    def near_point(value):
        return take_from(value, x_map=X_POINT)

    def near_target(value):
        return take_from(value, x_map=X_TARGET)

    def with_other(blocks):
        return blocks + [take_from(block, flip=1) for block in blocks]

    own = own_points
    beside, after, before = near_point(own), take_from(own, dz=1), take_from(own, dz=-1)
    near = [own, after, before, beside]
    beside_after, far = near_point(after), take_from(after, dz=1)
    beside_before = take_from(beside, dz=-1)

    target = own_targets
    t_beside, t_after = near_target(target), take_from(target, dy=1)
    t_before = take_from(target, dy=-1)
    first = with_other([target, t_beside, t_after, t_before])
    beside_far = take_from(beside_after, dz=1)
    t_beside_after, t_far = near_target(t_after), take_from(t_after, dy=1)
    t_beside_before = take_from(t_beside, dy=-1)

    half = project(near, weight, ())
    points = project([far, beside_after, beside_before, beside_far], weight, half)
    t_beside_after, t_far, t_beside_before, points = lax.optimization_barrier(
        (t_beside_after, t_far, t_beside_before, points)
    )
    t_beside_far = take_from(t_beside_after, dy=1)
    second = [t_beside_before, t_far, t_beside_after]
    third = [take_from(block, flip=1) for block in second]
    return points, first, second + [t_beside_far], third


def total_sum(place, kept, sent, local_loss):
    count, cut, lanes = kept.shape
    half = kept + take_from(sent, flip=1)
    own = jnp.sum(swap_blocks(half, same_core_group), axis=0)
    power = 14.0 - jnp.floor(jnp.log2(jnp.maximum(jnp.max(jnp.abs(own)), 1e-30)))
    small = (own * jnp.exp2(power)).astype(jnp.float16)
    first = (local_loss / 16.0).astype(jnp.float16)
    rest = local_loss - first.astype(jnp.float32) * 16.0
    second = (rest * 64.0).astype(jnp.float16)
    rest = rest - second.astype(jnp.float32) / 64.0
    third = (rest * 16384.0).astype(jnp.float16)
    values = [power.astype(jnp.float16), first, second, third]
    tail = jnp.stack([values[min(i, 3)] for i in range(8)])
    tail = jnp.broadcast_to(tail[:, None], (8, lanes))
    small = jnp.concatenate([small, tail], axis=0)
    here = swap_blocks(jnp.broadcast_to(small, (count,) + small.shape), same_core_group)
    there = take_from(here, flip=1)
    grad_w, loss = assemble(place, here.astype(jnp.float32), there.astype(jnp.float32))
    return grad_w, loss[0, 0]


def body(features, proj_weight, image_vals, image_scales, text_vals, text_scales, logit_scale):
    rows = features.shape[0]
    total = rows * lax.axis_size("row") * lax.axis_size("col")
    place = (lax.axis_index("row") % 2).astype(jnp.int32).reshape(1)

    own = unit_targets(image_vals, image_scales, text_vals, text_scales)
    (tile, proj, points), near, far, far_other = gather_and_project(features, own, proj_weight)
    turned = tile.T
    first, cols, diag, row_max, row_sum = logits_of(points, logit_scale, near, ())
    last, cols = lax.optimization_barrier((far[-1], cols))
    far = far[:-1] + [last] + far_other + [take_from(last, flip=1)]
    second, rows_part, cols_part = logits_of(points, logit_scale, far, (row_max, row_sum, cols))
    row_lse, col_lse = exchange_statistics(rows_part, cols_part)
    kept, sent, losses = grad_of(
        place,
        logit_scale,
        (first, second),
        near + far,
        row_lse,
        col_lse,
        diag,
        proj,
        turned,
    )
    grad_w, loss = total_sum(place, kept, sent, jnp.sum(losses[0]) * LN2)
    return (loss / (4.0 * total), grad_w)


def solution(mesh):
    return jax.shard_map(
        body,
        mesh=mesh,
        in_specs=(
            P(("row", "col"), None),
            P(),
            P(("row", "col"), None),
            P(("row", "col"), None),
            P(("row", "col"), None),
            P(("row", "col"), None),
            P(),
        ),
        out_specs=(P(), P()),
        check_vma=False,
    )
```

```python
import functools
import jax
import jax.numpy as jnp
from jax import lax
from jax.experimental import pallas as pl
from jax.experimental.pallas import tpu as pltpu
from jax.sharding import PartitionSpec as P

EPS = 1e-06
LOG2E = 1.4426950408889634
LN2 = 0.6931471805599453
SAFE = 60.0
AXES = ("row", "col")
X_POINT = (1, 0, 3, 2)
X_TARGET = (3, 2, 1, 0)
LANES = 128
WIDE = 2 * LANES
BATCHES = (((0, 0), (1, 0), (0, 1), (0, 3)), ((1, 3), (0, 2), (1, 1)), ((1, 2),))
ORDER = [(core,) + place for batch in BATCHES for core in range(2) for place in batch]
POINT_ORDER = (0, 1, 3, 4, 2, 5, 7, 6)


def device_index(x, y, z, core):
    row = ((x % 2) * 4 + y % 4) * 2 + core
    col = (x // 2) * 4 + z % 4
    return row * 8 + col


def take_from(value, x_map=None, dy=0, dz=0, flip=0):
    perm = []
    for x in range(4):
        source_x = x if x_map is None else x_map[x]
        for y in range(4):
            for z in range(4):
                for core in range(2):
                    source = device_index(source_x, y + dy, z + dz, core ^ flip)
                    perm.append((source, device_index(x, y, z, core)))
    return lax.ppermute(value, AXES, perm)


def whole():
    return pl.BlockSpec(memory_space=pltpu.VMEM)


def scalars():
    return pl.BlockSpec(memory_space=pltpu.SMEM)


def anywhere():
    return pl.BlockSpec(memory_space=pl.ANY)


def in_hbm():
    return pl.BlockSpec(memory_space=pltpu.HBM)


def params(mib, grid=False):
    return pltpu.CompilerParams(
        vmem_limit_bytes=mib * 2**20, **({"dimension_semantics": ("arbitrary",)} if grid else {})
    )


def canonical(block):
    core, flip, step = block
    return (core * 2 + flip) * 4 + step


def unit_kernel(image_ref, image_scale_ref, text_ref, text_scale_ref, out_ref):
    count, width = image_ref.shape
    blocks = image_scale_ref.shape[0]
    size = width // blocks
    for which, (vals, scales_ref) in enumerate(
        ((image_ref, image_scale_ref), (text_ref, text_scale_ref))
    ):
        scales = scales_ref[...].astype(jnp.float32)
        scales = jnp.concatenate([scales] * (count // blocks), axis=0).T
        full = [
            vals[:, k * size : (k + 1) * size].astype(jnp.float32) * scales[:, k : k + 1]
            for k in range(blocks)
        ]
        square = sum(jnp.sum(part * part, axis=-1, keepdims=True) for part in full)
        inv = lax.rsqrt(square + EPS)
        for k in range(blocks):
            out_ref[which * count : (which + 1) * count, k * size : (k + 1) * size] = (
                full[k] * inv
            ).astype(jnp.bfloat16)


def unit_targets(image_vals, image_scales, text_vals, text_scales):
    count, width = image_vals.shape
    return pl.pallas_call(
        unit_kernel,
        out_shape=jax.ShapeDtypeStruct((2 * count, width), jnp.bfloat16),
        in_specs=[whole()] * 4,
        out_specs=whole(),
        compiler_params=params(58),
        cost_estimate=pl.CostEstimate(flops=2**20, bytes_accessed=2**20, transcendentals=0),
    )(image_vals, image_scales.T, text_vals, text_scales.T)


def proj_kernel(*refs):
    feature_refs = refs[:4]
    weight_ref = refs[4]
    outs, (tile_ref, weight_in_ref, proj_ref, unit_ref, in_sem, out_sem) = refs[-9:-6], refs[-6:]
    base = 0 if len(refs) == 14 else tile_ref.shape[0]
    rows = feature_refs[0].shape[0]
    step = 2 * rows
    incoming = [pltpu.make_async_copy(weight_ref, weight_in_ref, in_sem.at[4])]
    for k in range(4):
        to = tile_ref.at[k * rows : (k + 1) * rows, :]
        incoming.append(pltpu.make_async_copy(feature_refs[k], to, in_sem.at[k]))
    for copy in incoming:
        copy.start()
    for copy in incoming:
        copy.wait()
    outgoing = []

    def send(held_ref, out_ref, at, count):
        copy = pltpu.make_async_copy(
            held_ref.at[at : at + count, :],
            out_ref.at[base + at : base + at + count, :],
            out_sem.at[len(outgoing)],
        )
        copy.start()
        outgoing.append(copy)

    send(tile_ref, outs[0], 0, 2 * step)
    for at in range(0, 2 * step, step):
        proj = jnp.dot(
            tile_ref[at : at + step, :], weight_in_ref[...], preferred_element_type=jnp.float32
        )
        inv = lax.rsqrt(jnp.sum(proj * proj, axis=-1, keepdims=True) + EPS)
        proj_ref[at : at + step, :] = proj
        unit_ref[at : at + step, :] = (proj * inv).astype(jnp.bfloat16)
        send(proj_ref, outs[1], at, step)
        send(unit_ref, outs[2], at, step)
    for copy in outgoing:
        copy.wait()


def project(features, weight, done):
    deep, width = weight.shape
    rows = 4 * features[0].shape[0]
    return pl.pallas_call(
        proj_kernel,
        out_shape=(
            jax.ShapeDtypeStruct((2 * rows, deep), jnp.bfloat16),
            jax.ShapeDtypeStruct((2 * rows, width), jnp.float32),
            jax.ShapeDtypeStruct((2 * rows, width), jnp.bfloat16),
        ),
        in_specs=[anywhere()] * 5 + [in_hbm(), in_hbm(), anywhere()][: len(done)],
        out_specs=(in_hbm(), in_hbm(), anywhere()),
        input_output_aliases={5 + k: k for k in range(len(done))},
        scratch_shapes=[
            pltpu.VMEM((rows, deep), jnp.bfloat16),
            pltpu.VMEM((deep, width), jnp.bfloat16),
            pltpu.VMEM((rows, width), jnp.float32),
            pltpu.VMEM((rows, width), jnp.bfloat16),
            pltpu.SemaphoreType.DMA((5,)),
            pltpu.SemaphoreType.DMA((5,)),
        ],
        compiler_params=params(20),
        cost_estimate=pl.CostEstimate(
            flops=2 * rows * deep * width, bytes_accessed=6 * 2**20, transcendentals=0
        ),
    )(*features, weight, *done)


def to_column(row):
    parts = []
    for at in range(0, row.shape[1], LANES):
        wide = jnp.broadcast_to(row[:, at : at + LANES], (LANES, LANES))
        parts.append(wide.T)
    return jnp.concatenate(parts, axis=0)


def logits_kernel(count, first, last, *refs):
    refs = list(refs)
    scale_ref, points_any = refs[:2]
    target_refs = refs[2 : 2 + count]
    rest = refs[2 + count : -7]
    olds = ()
    if not first:
        old_max_any, old_sum_any = rest[:2]
        old_max_ref, old_sum_ref = rest[-2:]
        olds = ((old_max_any, old_max_ref), (old_sum_any, old_sum_ref))
        rest = rest[2:-2]
    if last:
        old_col_refs = rest[:2]
        logits_ref, row_ref, all_col_ref, row_max_ref, row_sum_ref, col_ref = rest[2:]
    else:
        logits_ref, col_ref, diag_ref, row_max_ref, row_sum_ref = rest
    points_ref, targets_ref, held_ref, col_max_ref, weight_ref, out_sem, in_sem = refs[-7:]
    rows = points_ref.shape[0]
    chunk = 64
    scale = scale_ref[0] * LOG2E

    incoming = [pltpu.make_async_copy(points_any, points_ref, in_sem.at[count])]
    for j in range(count):
        to = targets_ref.at[j * WIDE : (j + 1) * WIDE, :]
        incoming.append(pltpu.make_async_copy(target_refs[j], to, in_sem.at[j]))
    for k, (source, to) in enumerate(olds):
        incoming.append(pltpu.make_async_copy(source, to, in_sem.at[count + 1 + k]))
    for copy in incoming:
        copy.start()
    incoming[0].wait()
    for copy in incoming[count + 1 :]:
        copy.wait()

    def copy_out(j):
        at = slice(j * WIDE, (j + 1) * WIDE)
        return pltpu.make_async_copy(held_ref.at[:, at], logits_ref.at[:, at], out_sem.at[j])

    for j in range(count):
        at = slice(j * WIDE, (j + 1) * WIDE)
        incoming[1 + j].wait()
        held_ref[:, at] = scale * lax.dot_general(
            points_ref[...],
            targets_ref[at, :],
            (((1,), (1,)), ((), ())),
            preferred_element_type=jnp.float32,
        )
        copy_out(j).start()
        top = None
        for r in range(0, rows, chunk):
            r_at = slice(r, r + chunk)
            value = held_ref[r_at, at]
            if j:
                row_max_ref[r_at, :] = jnp.maximum(row_max_ref[r_at, :], value)
            elif first:
                row_max_ref[r_at, :] = value
            else:
                row_max_ref[r_at, :] = jnp.maximum(old_max_ref[r_at, :], value)
            part = jnp.max(value.reshape(chunk // 8, 8, WIDE), axis=0)
            top = part if top is None else jnp.maximum(top, part)
        col_max_ref[j : j + 1, :] = jnp.max(top, axis=0, keepdims=True)

    peak = jnp.max(row_max_ref[...], axis=0, keepdims=True)
    near = jnp.min(col_max_ref[...] - peak) > -SAFE
    for r in range(0, rows, chunk):
        r_at = slice(r, r + chunk)
        weight_ref[r_at, :] = jnp.exp2(row_max_ref[r_at, :] - peak)
        if not first:
            shrink = jnp.exp2(old_max_ref[r_at, :] - row_max_ref[r_at, :])
            row_sum_ref[r_at, :] = old_sum_ref[r_at, :] * shrink
        else:
            row_sum_ref[r_at, :] = jnp.zeros((chunk, WIDE), jnp.float32)

    def finish(j, top, total):
        total = jnp.sum(total, axis=0, keepdims=True)
        col_ref[pl.ds(j, 1), :] = top + jnp.log(total) * LOG2E

    def near_sums(j, _):
        at = pl.ds(pl.multiple_of(j * WIDE, WIDE), WIDE)
        total = jnp.zeros((8, WIDE), jnp.float32)
        for r in range(0, rows, chunk):
            r_at = slice(r, r + chunk)
            part = jnp.exp2(held_ref[r_at, at] - row_max_ref[r_at, :])
            row_sum_ref[r_at, :] += part
            total += jnp.sum((part * weight_ref[r_at, :]).reshape(chunk // 8, 8, WIDE), axis=0)
        finish(j, peak, total)
        return 0

    def far_sums(j, _):
        at = pl.ds(pl.multiple_of(j * WIDE, WIDE), WIDE)
        top = col_max_ref[pl.ds(j, 1), :]
        total = jnp.zeros((8, WIDE), jnp.float32)
        for r in range(0, rows, chunk):
            r_at = slice(r, r + chunk)
            value = held_ref[r_at, at]
            row_sum_ref[r_at, :] += jnp.exp2(value - row_max_ref[r_at, :])
            total += jnp.sum(jnp.exp2(value - top).reshape(chunk // 8, 8, WIDE), axis=0)
        finish(j, top, total)
        return 0

    @pl.when(near)
    def _():
        lax.fori_loop(0, count, near_sums, 0)

    @pl.when(jnp.logical_not(near))
    def _():
        lax.fori_loop(0, count, far_sums, 0)

    if last:
        k = 0
        for source in (*old_col_refs, col_ref):
            for at in range(source.shape[0]):
                to = canonical(ORDER[k])
                all_col_ref[to : to + 1, :] = source[at : at + 1, :]
                k += 1
        for which in range(2):
            lanes = slice(which * LANES, (which + 1) * LANES)
            for k, place in enumerate(POINT_ORDER):
                r_at = slice(k * LANES, (k + 1) * LANES)
                tops = row_max_ref[r_at, lanes].T
                part = row_sum_ref[r_at, lanes].T
                top = jnp.max(tops, axis=0, keepdims=True)
                total = jnp.sum(part * jnp.exp2(tops - top), axis=0, keepdims=True)
                row_ref[which : which + 1, place * LANES : (place + 1) * LANES] = (
                    top + jnp.log(total) * LOG2E
                )
    else:
        rows_at = lax.broadcasted_iota(jnp.int32, (LANES, WIDE), 0)
        cols_at = lax.broadcasted_iota(jnp.int32, (LANES, WIDE), 1) % LANES
        own = jnp.where(rows_at == cols_at, held_ref[:LANES, :WIDE], 0.0)
        diag_ref[...] = jnp.broadcast_to(jnp.sum(own, axis=0, keepdims=True), diag_ref.shape)
    for j in range(count):
        copy_out(j).wait()


def logits_of(points, scale, targets, old, old_cols):
    rows, width = points.shape
    count = len(targets)
    cols = count * WIDE
    first, last = not old, bool(old_cols)
    lanes = (rows, WIDE)
    if last:
        shapes = [(2, rows), (16, WIDE)]
        held = [lanes, lanes, (count, WIDE)]
    else:
        shapes = [(count, WIDE), (8, WIDE), lanes, lanes]
        held = []
    held += [lanes] * len(old)
    return pl.pallas_call(
        functools.partial(logits_kernel, count, first, last),
        out_shape=[jax.ShapeDtypeStruct(shape, jnp.float32) for shape in [(rows, cols)] + shapes],
        in_specs=[scalars()]
        + [anywhere()] * (1 + count + len(old))
        + [whole()] * len(old_cols),
        out_specs=[in_hbm()] + [whole()] * len(shapes),
        scratch_shapes=[pltpu.VMEM(shape, jnp.float32) for shape in held]
        + [
            pltpu.VMEM((rows, width), jnp.bfloat16),
            pltpu.VMEM((cols, width), jnp.bfloat16),
            pltpu.VMEM((rows, cols), jnp.float32),
            pltpu.VMEM((count, WIDE), jnp.float32),
            pltpu.VMEM(lanes, jnp.float32),
            pltpu.SemaphoreType.DMA((count,)),
            pltpu.SemaphoreType.DMA((count + 3,)),
        ],
        compiler_params=params(28),
        cost_estimate=pl.CostEstimate(
            flops=2 * rows * cols * points.shape[1],
            bytes_accessed=4 * rows * cols,
            transcendentals=rows * cols,
        ),
    )(scale, points, *targets, *old, *old_cols)


def grad_kernel(place_ref, scale_ref, *refs):
    logits_refs = refs[:3]
    target_refs = refs[3:19]
    row_ref, all_col_ref, diag_ref, proj_ref, turned_any, kept_ref, sent_ref, loss_ref = refs[19:27]
    coef_ref, targets_ref, tops_ref, shares_ref, edges_ref, high_ref, low_ref = refs[27:34]
    part_ref, turned_ref, sem_ref = refs[34:]
    step = pl.program_id(0)
    size = proj_ref.shape[0]
    scale = scale_ref[0]
    chunk = 64

    def copy_in(k):
        if k == 16:
            return pltpu.make_async_copy(turned_any, turned_ref, sem_ref.at[k])
        return pltpu.make_async_copy(
            target_refs[k], targets_ref.at[k * WIDE : (k + 1) * WIDE, :], sem_ref.at[k]
        )

    peak = jnp.max(row_ref[...])
    near = peak - jnp.min(all_col_ref[...]) < SAFE

    @pl.when(step == 0)
    def _():
        for k in range(17):
            copy_in(k).start()
        for k, block in enumerate(ORDER):
            at = canonical(block)
            edges_ref[k : k + 1, :] = all_col_ref[at : at + 1, :]
        for k, place in enumerate(POINT_ORDER):
            for which in range(2):
                row = row_ref[which : which + 1, place * LANES : (place + 1) * LANES]
                r_at = slice(k * LANES, (k + 1) * LANES)
                lanes = slice(which * LANES, (which + 1) * LANES)
                tops_ref[r_at, lanes] = to_column(row)
                shares_ref[r_at, lanes] = to_column(jnp.exp2(row - peak))
        both = edges_ref[:1, :] - 2.0 * diag_ref[:1, :]
        both = both[:, :LANES] + both[:, LANES:] + row_ref[:1, :LANES] + row_ref[1:2, :LANES]
        loss_ref[...] = jnp.broadcast_to(both, loss_ref.shape)

    def own_hits(r):
        rows_at = lax.broadcasted_iota(jnp.int32, (chunk, WIDE), 0) + r + step * size
        cols_at = lax.broadcasted_iota(jnp.int32, (chunk, WIDE), 1) % LANES
        return jnp.where(rows_at == cols_at, 2.0, 0.0)

    def coefs(is_near):
        k = 0
        for logits_ref in logits_refs:
            for at in range(0, logits_ref.shape[1], WIDE):
                edge = edges_ref[k : k + 1, :]
                rise = jnp.exp2(peak - edge)
                for r in range(0, size, chunk):
                    value = logits_ref[r : r + chunk, at : at + WIDE]
                    r_at = pl.ds(pl.multiple_of(step * size + r, chunk), chunk)
                    coef = jnp.exp2(value - tops_ref[r_at, :])
                    if is_near:
                        coef = coef + coef * (shares_ref[r_at, :] * rise)
                    else:
                        coef = coef + jnp.exp2(value - edge)
                    if k == 0 and r < LANES:
                        coef = coef - own_hits(r)
                    coef_ref[r : r + chunk, k * WIDE : (k + 1) * WIDE] = coef.astype(jnp.bfloat16)
                k += 1

    @pl.when(near)
    def _():
        coefs(True)

    @pl.when(jnp.logical_not(near))
    def _():
        coefs(False)

    @pl.when(step == 0)
    def _():
        for k in range(16):
            copy_in(k).wait()

    grad = jnp.dot(coef_ref[...], targets_ref[...], preferred_element_type=jnp.float32)
    grad = grad * (scale * 0.25)
    proj = proj_ref[...]
    inv = lax.rsqrt(jnp.sum(proj * proj, axis=-1, keepdims=True) + EPS)
    along = jnp.sum(proj * grad, axis=-1, keepdims=True)
    grad = inv * (grad - along * inv * inv * proj)
    high = grad.astype(jnp.bfloat16)
    rows = pl.ds(pl.multiple_of(step * size, size), size)
    high_ref[rows, :] = high
    low_ref[rows, :] = (grad - high.astype(jnp.float32)).astype(jnp.bfloat16)

    @pl.when(step == pl.num_programs(0) - 1)
    def _():
        copy_in(16).wait()
        core = place_ref[0]
        deep = turned_ref.shape[0]
        cut = deep // 16

        def products(n, _):
            at = pl.ds(pl.multiple_of(n * WIDE, WIDE), WIDE)
            part_ref[...] = jnp.dot(
                turned_ref[...], high_ref[:, at], preferred_element_type=jnp.float32
            ) + jnp.dot(turned_ref[...], low_ref[:, at], preferred_element_type=jnp.float32)
            for v in range(8):
                for side in range(2):
                    lanes = slice(side * LANES, (side + 1) * LANES)
                    for out_ref, half in ((kept_ref, core), (sent_ref, 1 - core)):
                        from_row = pl.multiple_of(half * (deep // 2) + v * cut, 8)
                        out_ref[v * 8 + 2 * n + side] = part_ref[pl.ds(from_row, cut), lanes]
            return 0

        lax.fori_loop(0, high_ref.shape[1] // WIDE, products, 0)


def grad_of(place, scale, logits, targets, row_lse, col_lse, diag, proj, turned):
    rows, width = proj.shape
    deep = turned.shape[0]
    step = 256
    cut = deep // 16
    piece = jax.ShapeDtypeStruct((64, cut, LANES), jnp.float32)
    cols = sum(part.shape[1] for part in logits)
    return pl.pallas_call(
        grad_kernel,
        grid=(rows // step,),
        out_shape=(piece, piece, jax.ShapeDtypeStruct((8, LANES), jnp.float32)),
        in_specs=[scalars(), scalars()]
        + [pl.BlockSpec((step, part.shape[1]), lambda i: (i, 0)) for part in logits]
        + [anywhere()] * len(targets)
        + [whole(), whole(), whole()]
        + [pl.BlockSpec((step, width), lambda i: (i, 0)), anywhere()],
        out_specs=(whole(), whole(), whole()),
        scratch_shapes=[
            pltpu.VMEM((step, cols), jnp.bfloat16),
            pltpu.VMEM((cols, width), jnp.bfloat16),
            pltpu.VMEM((rows, WIDE), jnp.float32),
            pltpu.VMEM((rows, WIDE), jnp.float32),
            pltpu.VMEM((16, WIDE), jnp.float32),
            pltpu.VMEM((rows, width), jnp.bfloat16),
            pltpu.VMEM((rows, width), jnp.bfloat16),
            pltpu.VMEM((deep, WIDE), jnp.float32),
            pltpu.VMEM((deep, rows), jnp.bfloat16),
            pltpu.SemaphoreType.DMA((len(targets) + 1,)),
        ],
        compiler_params=params(36, True),
        cost_estimate=pl.CostEstimate(
            flops=2 * rows * cols * width, bytes_accessed=32 * 2**20, transcendentals=rows * cols
        ),
    )(place, scale, *logits, *targets, row_lse, col_lse, diag, proj, turned)


def assemble_kernel(place_ref, here_ref, there_ref, out_ref, loss_ref, held_ref, sem_ref):
    cut = here_ref.shape[1] - 8
    half = 8 * cut
    copies = []
    loss = jnp.zeros((1, LANES), jnp.float32)
    for turn, ref in enumerate((here_ref, there_ref)):
        from_row = pl.multiple_of((place_ref[0] ^ turn) * half, 8)
        for v in range(8):
            for w in range(8):
                flags = [ref[v * 8 + w, cut + k : cut + k + 1, :] for k in range(4)]
                held_ref[turn, v * cut : (v + 1) * cut, w * LANES : (w + 1) * LANES] = ref[
                    v * 8 + w, :cut
                ] * jnp.exp2(-flags[0])
                loss += flags[1] * 16.0 + flags[2] / 64.0 + flags[3] / 16384.0
        copy = pltpu.make_async_copy(
            held_ref.at[turn], out_ref.at[pl.ds(from_row, half), :], sem_ref.at[turn]
        )
        copy.start()
        copies.append(copy)
    loss_ref[...] = jnp.broadcast_to(loss, loss_ref.shape)
    for copy in copies:
        copy.wait()


def assemble(place, here, there):
    cut = here.shape[1] - 8
    return pl.pallas_call(
        assemble_kernel,
        in_specs=[scalars(), whole(), whole()],
        out_specs=(anywhere(), whole()),
        out_shape=(
            jax.ShapeDtypeStruct((16 * cut, 8 * LANES), jnp.float32),
            jax.ShapeDtypeStruct((8, LANES), jnp.float32),
        ),
        scratch_shapes=[
            pltpu.VMEM((2, 8 * cut, 8 * LANES), jnp.float32),
            pltpu.SemaphoreType.DMA((2,)),
        ],
        compiler_params=params(16),
        cost_estimate=pl.CostEstimate(flops=2**20, bytes_accessed=9 * 2**20, transcendentals=0),
    )(place, here, there)


def same_core_group(x, y, z, core):
    return (core,), (x, y, z)


def groups_of(rule):
    found = {}
    for x in range(4):
        for y in range(4):
            for z in range(4):
                for core in range(2):
                    group, place = rule(x, y, z, core)
                    found.setdefault(group, []).append((place, device_index(x, y, z, core)))
    return [[device for _, device in sorted(found[group])] for group in sorted(found)]


def swap_blocks(value, rule):
    return lax.all_to_all(
        value, AXES, split_axis=0, concat_axis=0, axis_index_groups=groups_of(rule), tiled=True
    )


def merged(value, got):
    low, high = jnp.minimum(value, got), jnp.maximum(value, got)
    return high + jnp.log(1.0 + jnp.exp2(low - high)) * LOG2E


def exchange_statistics(rows, cols):
    row_shape = (2, 2, 4, rows.shape[1] // 8)
    col_shape = (2, 2, 4, cols.shape[1])

    def row_add(value, got):
        return merged(value, got.reshape(rows.shape))

    def col_add(value, got):
        return merged(value, got.reshape(cols.shape))

    got_rows = take_from(rows, x_map=X_POINT)
    got_cols = take_from(cols, flip=1)
    rows = row_add(rows, got_rows.reshape(row_shape)[:, ::-1])
    cols = col_add(cols, got_cols.reshape(col_shape)[::-1])
    rows, cols = lax.optimization_barrier((rows, cols))
    got_rows = take_from(rows, dz=1)
    got_cols = take_from(cols, x_map=X_TARGET)
    rows = row_add(rows, jnp.roll(got_rows.reshape(row_shape), 1, axis=2))
    cols = col_add(cols, got_cols.reshape(col_shape)[:, ::-1])
    rows, cols = lax.optimization_barrier((rows, cols))
    got_rows = take_from(rows, dz=2)
    got_cols = take_from(cols, dy=1)
    rows = row_add(rows, jnp.roll(got_rows.reshape(row_shape), 2, axis=2))
    cols = col_add(cols, jnp.roll(got_cols.reshape(col_shape), 1, axis=2))
    got_cols = take_from(cols, dy=2)
    return rows, col_add(cols, jnp.roll(got_cols.reshape(col_shape), 2, axis=2))


def gather_and_project(own_points, own_targets, weight):
    def near_point(value):
        return take_from(value, x_map=X_POINT)

    def near_target(value):
        return take_from(value, x_map=X_TARGET)

    own = own_points
    beside, after, before = near_point(own), take_from(own, dz=1), take_from(own, dz=-1)
    beside, after, before, target = lax.optimization_barrier((beside, after, before, own_targets))
    near = [own, after, before, beside]
    beside_after, far = near_point(after), take_from(after, dz=1)
    beside_before = take_from(beside, dz=-1)
    t_beside, t_after = near_target(target), take_from(target, dy=1)

    t_before = take_from(target, dy=-1)
    beside_far = take_from(beside_after, dz=1)
    half = project(near, weight, ())
    t_beside, t_after, beside_far, half = lax.optimization_barrier(
        (t_beside, t_after, beside_far, half)
    )
    t_beside_after, t_far = near_target(t_after), take_from(t_after, dy=1)
    t_beside_before = take_from(t_beside, dy=-1)
    points = project([far, beside_after, beside_before, beside_far], weight, half)
    first = [target, t_beside, t_after, t_before]
    return points, first, [t_beside_before, t_far, t_beside_after]


def with_other(blocks):
    return blocks + [take_from(block, flip=1) for block in blocks]


def total_sum(place, kept, sent, local_loss):
    count, cut, lanes = kept.shape
    half = kept + take_from(sent, flip=1)
    own = jnp.sum(swap_blocks(half, same_core_group), axis=0)
    power = 14.0 - jnp.floor(jnp.log2(jnp.maximum(jnp.max(jnp.abs(own)), 1e-30)))
    small = (own * jnp.exp2(power)).astype(jnp.float16)
    first = (local_loss / 16.0).astype(jnp.float16)
    rest = local_loss - first.astype(jnp.float32) * 16.0
    second = (rest * 64.0).astype(jnp.float16)
    rest = rest - second.astype(jnp.float32) / 64.0
    third = (rest * 16384.0).astype(jnp.float16)
    values = [power.astype(jnp.float16), first, second, third]
    tail = jnp.stack([values[min(i, 3)] for i in range(8)])
    tail = jnp.broadcast_to(tail[:, None], (8, lanes))
    small = jnp.concatenate([small, tail], axis=0)
    here = swap_blocks(jnp.broadcast_to(small, (count,) + small.shape), same_core_group)
    there = take_from(here, flip=1)
    grad_w, loss = assemble(place, here.astype(jnp.float32), there.astype(jnp.float32))
    return grad_w, loss[0, 0]


def body(features, proj_weight, image_vals, image_scales, text_vals, text_scales, logit_scale):
    rows = features.shape[0]
    total = rows * lax.axis_size("row") * lax.axis_size("col")
    place = (lax.axis_index("row") % 2).astype(jnp.int32).reshape(1)

    own = unit_targets(image_vals, image_scales, text_vals, text_scales)
    (tile, proj, points), near, far = gather_and_project(features, own, proj_weight)
    turned = tile.T
    near = with_other(near)
    first, near_cols, diag, *old = logits_of(points, logit_scale, near, (), ())
    far, near_cols = lax.optimization_barrier((far, near_cols))
    last = take_from(far[-1], dy=1)
    far = with_other(far)
    second, far_cols, _, *old = logits_of(points, logit_scale, far, old, ())
    last, far_cols = lax.optimization_barrier((last, far_cols))
    last = with_other([last])
    third, rows_part, cols_part = logits_of(
        points, logit_scale, last, old, (near_cols, far_cols)
    )
    row_lse, col_lse = exchange_statistics(rows_part, cols_part)
    kept, sent, losses = grad_of(
        place,
        logit_scale,
        (first, second, third),
        near + far + last,
        row_lse,
        col_lse,
        diag,
        proj,
        turned,
    )
    grad_w, loss = total_sum(place, kept, sent, jnp.sum(losses[0]) * LN2)
    return (loss / (4.0 * total), grad_w)


def solution(mesh):
    return jax.shard_map(
        body,
        mesh=mesh,
        in_specs=(
            P(("row", "col"), None),
            P(),
            P(("row", "col"), None),
            P(("row", "col"), None),
            P(("row", "col"), None),
            P(("row", "col"), None),
            P(),
        ),
        out_specs=(P(), P()),
        check_vma=False,
    )
```

```python
import functools
import jax
import jax.numpy as jnp
from jax import lax
from jax.experimental import pallas as pl
from jax.experimental.pallas import tpu as pltpu
from jax.sharding import PartitionSpec as P

EPS = 1e-06
LOG2E = 1.4426950408889634
LN2 = 0.6931471805599453
SAFE = 60.0
AXES = ("row", "col")
X_POINT = (1, 0, 3, 2)
X_TARGET = (3, 2, 1, 0)
LANES = 128
WIDE = 2 * LANES
BATCHES = (((0, 0), (1, 0), (0, 1), (0, 3)), ((1, 3), (0, 2), (1, 1)), ((1, 2),))
ORDER = [(core,) + place for batch in BATCHES for core in range(2) for place in batch]
POINT_ORDER = tuple(range(8))


def device_index(x, y, z, core):
    row = ((x % 2) * 4 + y % 4) * 2 + core
    col = (x // 2) * 4 + z % 4
    return row * 8 + col


def take_from(value, x_map=None, dy=0, dz=0, flip=0):
    perm = []
    for x in range(4):
        source_x = x if x_map is None else x_map[x]
        for y in range(4):
            for z in range(4):
                for core in range(2):
                    source = device_index(source_x, y + dy, z + dz, core ^ flip)
                    perm.append((source, device_index(x, y, z, core)))
    return lax.ppermute(value, AXES, perm)


def whole():
    return pl.BlockSpec(memory_space=pltpu.VMEM)


def scalars():
    return pl.BlockSpec(memory_space=pltpu.SMEM)


def anywhere():
    return pl.BlockSpec(memory_space=pl.ANY)


def params(mib, grid=False):
    return pltpu.CompilerParams(
        vmem_limit_bytes=mib * 2**20, **({"dimension_semantics": ("arbitrary",)} if grid else {})
    )


def canonical(block):
    core, flip, step = block
    return (core * 2 + flip) * 4 + step


def unit_kernel(image_ref, image_scale_ref, text_ref, text_scale_ref, out_ref):
    count, width = image_ref.shape
    blocks = image_scale_ref.shape[0]
    size = width // blocks
    for which, (vals, scales_ref) in enumerate(
        ((image_ref, image_scale_ref), (text_ref, text_scale_ref))
    ):
        scales = scales_ref[...].astype(jnp.float32)
        scales = jnp.concatenate([scales] * (count // blocks), axis=0).T
        full = [
            vals[:, k * size : (k + 1) * size].astype(jnp.float32) * scales[:, k : k + 1]
            for k in range(blocks)
        ]
        square = sum(jnp.sum(part * part, axis=-1, keepdims=True) for part in full)
        inv = lax.rsqrt(square + EPS)
        for k in range(blocks):
            out_ref[which * count : (which + 1) * count, k * size : (k + 1) * size] = (
                full[k] * inv
            ).astype(jnp.bfloat16)


def unit_targets(image_vals, image_scales, text_vals, text_scales):
    count, width = image_vals.shape
    return pl.pallas_call(
        unit_kernel,
        out_shape=jax.ShapeDtypeStruct((2 * count, width), jnp.bfloat16),
        in_specs=[whole()] * 4,
        out_specs=whole(),
        compiler_params=params(58),
        cost_estimate=pl.CostEstimate(flops=2**20, bytes_accessed=2**20, transcendentals=0),
    )(image_vals, image_scales.T, text_vals, text_scales.T)


def proj_kernel(*refs):
    feature_refs = refs[:8]
    weight_ref, tile_ref, proj_ref, unit_ref = refs[8:]
    step = pl.program_id(0)
    rows = feature_refs[0].shape[0]
    for turn in range(2):

        @pl.when(step == turn)
        def _():
            for k in range(4):
                tile_ref[k * rows : (k + 1) * rows, :] = feature_refs[4 * turn + k][...]

    proj = jnp.dot(tile_ref[...], weight_ref[...], preferred_element_type=jnp.float32)
    inv = lax.rsqrt(jnp.sum(proj * proj, axis=-1, keepdims=True) + EPS)
    proj_ref[...] = proj
    unit_ref[...] = (proj * inv).astype(jnp.bfloat16)


def project(features, weight):
    deep, width = weight.shape
    step = 4 * features[0].shape[0]
    once = pl.Buffered(1)

    def rows_of(array_width):
        return pl.BlockSpec((step, array_width), lambda i: (i, 0))

    return pl.pallas_call(
        proj_kernel,
        grid=(2,),
        out_shape=(
            jax.ShapeDtypeStruct((2 * step, deep), jnp.bfloat16),
            jax.ShapeDtypeStruct((2 * step, width), jnp.float32),
            jax.ShapeDtypeStruct((2 * step, width), jnp.bfloat16),
        ),
        in_specs=[pl.BlockSpec(part.shape, lambda i: (0, 0), pipeline_mode=once) for part in features]
        + [pl.BlockSpec((deep, width), lambda i: (0, 0), pipeline_mode=once)],
        out_specs=(rows_of(deep), rows_of(width), rows_of(width)),
        compiler_params=params(58, True),
        cost_estimate=pl.CostEstimate(
            flops=4 * step * deep * width, bytes_accessed=12 * 2**20, transcendentals=0
        ),
    )(*features, weight)


def to_column(row):
    parts = []
    for at in range(0, row.shape[1], LANES):
        wide = jnp.broadcast_to(row[:, at : at + LANES], (LANES, LANES))
        parts.append(wide.T)
    return jnp.concatenate(parts, axis=0)


def logits_kernel(count, first, last, *refs):
    refs = list(refs)
    scale_ref, points_ref = refs[:2]
    target_refs = refs[2 : 2 + count]
    refs = refs[2 + count :]
    if not first:
        old_max_ref, old_sum_ref = refs[:2]
        refs = refs[2:]
    if last:
        old_col_refs = refs[:2]
        refs = refs[2:]
    logits_ref, col_ref = refs[:2]
    refs = refs[2:]
    if first:
        diag_ref = refs.pop(0)
    if last:
        row_ref, all_col_ref = refs[:2]
        refs = refs[2:]
    row_max_ref, row_sum_ref, held_ref, col_max_ref, sem_ref = refs
    rows = points_ref.shape[0]
    chunk = 64
    scale = scale_ref[0] * LOG2E

    def copy_out(j):
        at = slice(j * WIDE, (j + 1) * WIDE)
        return pltpu.make_async_copy(held_ref.at[:, at], logits_ref.at[:, at], sem_ref.at[j])

    for j in range(count):
        at = slice(j * WIDE, (j + 1) * WIDE)
        held_ref[:, at] = scale * lax.dot_general(
            points_ref[...],
            target_refs[j][...],
            (((1,), (1,)), ((), ())),
            preferred_element_type=jnp.float32,
        )
        copy_out(j).start()
        top = None
        for r in range(0, rows, chunk):
            value = held_ref[r : r + chunk, at]
            if j:
                row_max_ref[r : r + chunk, :] = jnp.maximum(row_max_ref[r : r + chunk, :], value)
            elif first:
                row_max_ref[r : r + chunk, :] = value
            else:
                row_max_ref[r : r + chunk, :] = jnp.maximum(old_max_ref[r : r + chunk, :], value)
            part = jnp.max(value.reshape(chunk // 8, 8, WIDE), axis=0)
            top = part if top is None else jnp.maximum(top, part)
        col_max_ref[j : j + 1, :] = jnp.max(top, axis=0, keepdims=True)

    if first:
        rows_at = lax.broadcasted_iota(jnp.int32, (LANES, WIDE), 0)
        cols_at = lax.broadcasted_iota(jnp.int32, (LANES, WIDE), 1) % LANES
        own = jnp.where(rows_at == cols_at, held_ref[:LANES, :WIDE], 0.0)
        diag_ref[...] = jnp.broadcast_to(jnp.sum(own, axis=0, keepdims=True), diag_ref.shape)
        row_sum_ref[...] = jnp.zeros(row_sum_ref.shape, jnp.float32)
    else:
        row_sum_ref[...] = old_sum_ref[...] * jnp.exp2(old_max_ref[...] - row_max_ref[...])

    def sums(j, _):
        at = pl.ds(pl.multiple_of(j * WIDE, WIDE), WIDE)
        top = col_max_ref[pl.ds(j, 1), :]
        total = jnp.zeros((8, WIDE), jnp.float32)
        for r in range(0, rows, chunk):
            value = held_ref[r : r + chunk, at]
            row_sum_ref[r : r + chunk, :] += jnp.exp2(value - row_max_ref[r : r + chunk, :])
            total += jnp.sum(jnp.exp2(value - top).reshape(chunk // 8, 8, WIDE), axis=0)
        col_ref[pl.ds(j, 1), :] = top + jnp.log(jnp.sum(total, axis=0, keepdims=True)) * LOG2E
        return 0

    lax.fori_loop(0, count, sums, 0)
    if last:
        k = 0
        for source in (*old_col_refs, col_ref):
            for at in range(source.shape[0]):
                to = canonical(ORDER[k])
                all_col_ref[to : to + 1, :] = source[at : at + 1, :]
                k += 1
        for which in range(2):
            lanes = slice(which * LANES, (which + 1) * LANES)
            for r in range(0, rows, LANES):
                tops = row_max_ref[r : r + LANES, lanes].T
                part = row_sum_ref[r : r + LANES, lanes].T
                top = jnp.max(tops, axis=0, keepdims=True)
                total = jnp.sum(part * jnp.exp2(tops - top), axis=0, keepdims=True)
                row_ref[which : which + 1, r : r + LANES] = top + jnp.log(total) * LOG2E
    for j in range(count):
        copy_out(j).wait()


def logits_of(points, scale, targets, old, old_cols):
    rows = points.shape[0]
    count = len(targets)
    cols = count * WIDE
    first, last = not old, bool(old_cols)
    lanes = jax.ShapeDtypeStruct((rows, WIDE), jnp.float32)
    held = [pltpu.VMEM(lanes.shape, jnp.float32)] * 2
    outs = [
        jax.ShapeDtypeStruct((rows, cols), jnp.float32),
        jax.ShapeDtypeStruct((count, WIDE), jnp.float32),
    ]
    if first:
        outs.append(jax.ShapeDtypeStruct((8, WIDE), jnp.float32))
    if last:
        outs.append(jax.ShapeDtypeStruct((2, rows), jnp.float32))
        outs.append(jax.ShapeDtypeStruct((16, WIDE), jnp.float32))
    else:
        outs += [lanes, lanes]
    return pl.pallas_call(
        functools.partial(logits_kernel, count, first, last),
        out_shape=outs,
        in_specs=[scalars()] + [whole()] * (1 + count + len(old) + len(old_cols)),
        out_specs=[pl.BlockSpec(memory_space=pl.ANY)] + [whole()] * (len(outs) - 1),
        scratch_shapes=(held if last else [])
        + [
            pltpu.VMEM((rows, cols), jnp.float32),
            pltpu.VMEM((count, WIDE), jnp.float32),
            pltpu.SemaphoreType.DMA((count,)),
        ],
        compiler_params=params(58),
        cost_estimate=pl.CostEstimate(
            flops=2 * rows * cols * points.shape[1],
            bytes_accessed=4 * rows * cols,
            transcendentals=2 * rows * cols,
        ),
    )(scale, points, *targets, *old, *old_cols)


def grad_kernel(place_ref, scale_ref, *refs):
    logits_refs = refs[:3]
    target_refs = refs[3:19]
    row_ref, all_col_ref, diag_ref, proj_ref, turned_any, kept_ref, sent_ref, loss_ref = refs[19:27]
    coef_ref, targets_ref, tops_ref, shares_ref, edges_ref, high_ref, low_ref = refs[27:34]
    part_ref, turned_ref, sem_ref = refs[34:]
    step = pl.program_id(0)
    size = proj_ref.shape[0]
    scale = scale_ref[0]
    chunk = 64

    def copy_in(k):
        if k == 16:
            return pltpu.make_async_copy(turned_any, turned_ref, sem_ref.at[k])
        return pltpu.make_async_copy(
            target_refs[k], targets_ref.at[k * WIDE : (k + 1) * WIDE, :], sem_ref.at[k]
        )

    peak = jnp.max(row_ref[...])
    near = peak - jnp.min(all_col_ref[...]) < SAFE

    @pl.when(step == 0)
    def _():
        for k in range(17):
            copy_in(k).start()
        for k, block in enumerate(ORDER):
            at = canonical(block)
            edges_ref[k : k + 1, :] = all_col_ref[at : at + 1, :]
        for k, place in enumerate(POINT_ORDER):
            for which in range(2):
                row = row_ref[which : which + 1, place * LANES : (place + 1) * LANES]
                r_at = slice(k * LANES, (k + 1) * LANES)
                lanes = slice(which * LANES, (which + 1) * LANES)
                tops_ref[r_at, lanes] = to_column(row)
                shares_ref[r_at, lanes] = to_column(jnp.exp2(row - peak))
        both = edges_ref[:1, :] - 2.0 * diag_ref[:1, :]
        both = both[:, :LANES] + both[:, LANES:] + row_ref[:1, :LANES] + row_ref[1:2, :LANES]
        loss_ref[...] = jnp.broadcast_to(both, loss_ref.shape)

    def own_hits(r):
        rows_at = lax.broadcasted_iota(jnp.int32, (chunk, WIDE), 0) + r + step * size
        cols_at = lax.broadcasted_iota(jnp.int32, (chunk, WIDE), 1) % LANES
        return jnp.where(rows_at == cols_at, 2.0, 0.0)

    def coefs(is_near):
        k = 0
        for logits_ref in logits_refs:
            for at in range(0, logits_ref.shape[1], WIDE):
                edge = edges_ref[k : k + 1, :]
                rise = jnp.exp2(peak - edge)
                for r in range(0, size, chunk):
                    value = logits_ref[r : r + chunk, at : at + WIDE]
                    r_at = pl.ds(pl.multiple_of(step * size + r, chunk), chunk)
                    coef = jnp.exp2(value - tops_ref[r_at, :])
                    if is_near:
                        coef = coef + coef * (shares_ref[r_at, :] * rise)
                    else:
                        coef = coef + jnp.exp2(value - edge)
                    if k == 0 and r < LANES:
                        coef = coef - own_hits(r)
                    coef_ref[r : r + chunk, k * WIDE : (k + 1) * WIDE] = coef.astype(jnp.bfloat16)
                k += 1

    @pl.when(near)
    def _():
        coefs(True)

    @pl.when(jnp.logical_not(near))
    def _():
        coefs(False)

    @pl.when(step == 0)
    def _():
        for k in range(16):
            copy_in(k).wait()

    grad = jnp.dot(coef_ref[...], targets_ref[...], preferred_element_type=jnp.float32)
    grad = grad * (scale * 0.25)
    proj = proj_ref[...]
    inv = lax.rsqrt(jnp.sum(proj * proj, axis=-1, keepdims=True) + EPS)
    along = jnp.sum(proj * grad, axis=-1, keepdims=True)
    grad = inv * (grad - along * inv * inv * proj)
    high = grad.astype(jnp.bfloat16)
    rows = pl.ds(pl.multiple_of(step * size, size), size)
    high_ref[rows, :] = high
    low_ref[rows, :] = (grad - high.astype(jnp.float32)).astype(jnp.bfloat16)

    @pl.when(step == pl.num_programs(0) - 1)
    def _():
        copy_in(16).wait()
        core = place_ref[0]
        deep = turned_ref.shape[0]
        cut = deep // 16

        def products(n, _):
            at = pl.ds(pl.multiple_of(n * WIDE, WIDE), WIDE)
            part_ref[...] = jnp.dot(
                turned_ref[...], high_ref[:, at], preferred_element_type=jnp.float32
            ) + jnp.dot(turned_ref[...], low_ref[:, at], preferred_element_type=jnp.float32)
            for v in range(8):
                for side in range(2):
                    lanes = slice(side * LANES, (side + 1) * LANES)
                    for out_ref, half in ((kept_ref, core), (sent_ref, 1 - core)):
                        from_row = pl.multiple_of(half * (deep // 2) + v * cut, 8)
                        out_ref[v * 8 + 2 * n + side] = part_ref[pl.ds(from_row, cut), lanes]
            return 0

        lax.fori_loop(0, high_ref.shape[1] // WIDE, products, 0)


def grad_of(place, scale, logits, targets, row_lse, col_lse, diag, proj, turned):
    rows, width = proj.shape
    deep = turned.shape[0]
    step = 256
    cut = deep // 16
    piece = jax.ShapeDtypeStruct((64, cut, LANES), jnp.float32)
    cols = sum(part.shape[1] for part in logits)
    return pl.pallas_call(
        grad_kernel,
        grid=(rows // step,),
        out_shape=(piece, piece, jax.ShapeDtypeStruct((8, LANES), jnp.float32)),
        in_specs=[scalars(), scalars()]
        + [pl.BlockSpec((step, part.shape[1]), lambda i: (i, 0)) for part in logits]
        + [anywhere()] * len(targets)
        + [whole(), whole(), whole()]
        + [pl.BlockSpec((step, width), lambda i: (i, 0)), anywhere()],
        out_specs=(whole(), whole(), whole()),
        scratch_shapes=[
            pltpu.VMEM((step, cols), jnp.bfloat16),
            pltpu.VMEM((cols, width), jnp.bfloat16),
            pltpu.VMEM((rows, WIDE), jnp.float32),
            pltpu.VMEM((rows, WIDE), jnp.float32),
            pltpu.VMEM((16, WIDE), jnp.float32),
            pltpu.VMEM((rows, width), jnp.bfloat16),
            pltpu.VMEM((rows, width), jnp.bfloat16),
            pltpu.VMEM((deep, WIDE), jnp.float32),
            pltpu.VMEM((deep, rows), jnp.bfloat16),
            pltpu.SemaphoreType.DMA((len(targets) + 1,)),
        ],
        compiler_params=params(58, True),
        cost_estimate=pl.CostEstimate(
            flops=2 * rows * cols * width, bytes_accessed=32 * 2**20, transcendentals=rows * cols
        ),
    )(place, scale, *logits, *targets, row_lse, col_lse, diag, proj, turned)


def assemble_kernel(place_ref, here_ref, there_ref, out_ref, loss_ref, held_ref, sem_ref):
    cut = here_ref.shape[1] - 8
    half = 8 * cut
    copies = []
    loss = jnp.zeros((1, LANES), jnp.float32)
    for turn, ref in enumerate((here_ref, there_ref)):
        from_row = pl.multiple_of((place_ref[0] ^ turn) * half, 8)
        for v in range(8):
            for w in range(8):
                flags = [ref[v * 8 + w, cut + k : cut + k + 1, :] for k in range(4)]
                held_ref[turn, v * cut : (v + 1) * cut, w * LANES : (w + 1) * LANES] = ref[
                    v * 8 + w, :cut
                ] * jnp.exp2(-flags[0])
                loss += flags[1] * 16.0 + flags[2] / 64.0 + flags[3] / 16384.0
        copy = pltpu.make_async_copy(
            held_ref.at[turn], out_ref.at[pl.ds(from_row, half), :], sem_ref.at[turn]
        )
        copy.start()
        copies.append(copy)
    loss_ref[...] = jnp.broadcast_to(loss, loss_ref.shape)
    for copy in copies:
        copy.wait()


def assemble(place, here, there):
    cut = here.shape[1] - 8
    return pl.pallas_call(
        assemble_kernel,
        in_specs=[scalars(), whole(), whole()],
        out_specs=(anywhere(), whole()),
        out_shape=(
            jax.ShapeDtypeStruct((16 * cut, 8 * LANES), jnp.float32),
            jax.ShapeDtypeStruct((8, LANES), jnp.float32),
        ),
        scratch_shapes=[
            pltpu.VMEM((2, 8 * cut, 8 * LANES), jnp.float32),
            pltpu.SemaphoreType.DMA((2,)),
        ],
        compiler_params=params(16),
        cost_estimate=pl.CostEstimate(flops=2**20, bytes_accessed=9 * 2**20, transcendentals=0),
    )(place, here, there)


def same_core_group(x, y, z, core):
    return (core,), (x, y, z)


def groups_of(rule):
    found = {}
    for x in range(4):
        for y in range(4):
            for z in range(4):
                for core in range(2):
                    group, place = rule(x, y, z, core)
                    found.setdefault(group, []).append((place, device_index(x, y, z, core)))
    return [[device for _, device in sorted(found[group])] for group in sorted(found)]


def swap_blocks(value, rule):
    return lax.all_to_all(
        value, AXES, split_axis=0, concat_axis=0, axis_index_groups=groups_of(rule), tiled=True
    )


def merged(value, got):
    low, high = jnp.minimum(value, got), jnp.maximum(value, got)
    return high + jnp.log(1.0 + jnp.exp2(low - high)) * LOG2E


def exchange_statistics(rows, cols):
    row_shape = (2, 2, 4, rows.shape[1] // 8)
    col_shape = (2, 2, 4, cols.shape[1])

    def row_add(value, got):
        return merged(value, got.reshape(rows.shape))

    def col_add(value, got):
        return merged(value, got.reshape(cols.shape))

    got_rows = take_from(rows, x_map=X_POINT)
    got_cols = take_from(cols, flip=1)
    rows = row_add(rows, got_rows.reshape(row_shape)[:, ::-1])
    cols = col_add(cols, got_cols.reshape(col_shape)[::-1])
    rows, cols = lax.optimization_barrier((rows, cols))
    got_rows = take_from(rows, dz=1)
    got_cols = take_from(cols, x_map=X_TARGET)
    rows = row_add(rows, jnp.roll(got_rows.reshape(row_shape), 1, axis=2))
    cols = col_add(cols, got_cols.reshape(col_shape)[:, ::-1])
    rows, cols = lax.optimization_barrier((rows, cols))
    got_rows = take_from(rows, dz=2)
    got_cols = take_from(cols, dy=1)
    rows = row_add(rows, jnp.roll(got_rows.reshape(row_shape), 2, axis=2))
    cols = col_add(cols, jnp.roll(got_cols.reshape(col_shape), 1, axis=2))
    got_cols = take_from(cols, dy=2)
    return rows, col_add(cols, jnp.roll(got_cols.reshape(col_shape), 2, axis=2))


def gather_points(own):
    def near(value):
        return take_from(value, x_map=X_POINT)

    beside, after, before = near(own), take_from(own, dz=1), take_from(own, dz=-1)
    beside_before, far, beside_after = take_from(beside, dz=-1), take_from(after, dz=1), near(after)
    beside_far = take_from(beside_after, dz=1)
    return [own, after, far, before, beside, beside_after, beside_far, beside_before]


def gather_targets(own):
    def near(value):
        return take_from(value, x_map=X_TARGET)

    def with_other(blocks):
        return blocks + [take_from(block, flip=1) for block in blocks]

    beside, after, before = near(own), take_from(own, dy=1), take_from(own, dy=-1)
    first = with_other([own, beside, after, before])
    beside_before, far, beside_after = take_from(beside, dy=-1), take_from(after, dy=1), near(after)
    second = with_other([beside_before, far, beside_after])
    third = with_other([take_from(beside_after, dy=1)])
    return [first, second, third]


def total_sum(place, kept, sent, local_loss):
    count, cut, lanes = kept.shape
    half = kept + take_from(sent, flip=1)
    own = jnp.sum(swap_blocks(half, same_core_group), axis=0)
    power = 14.0 - jnp.floor(jnp.log2(jnp.maximum(jnp.max(jnp.abs(own)), 1e-30)))
    small = (own * jnp.exp2(power)).astype(jnp.float16)
    first = (local_loss / 16.0).astype(jnp.float16)
    rest = local_loss - first.astype(jnp.float32) * 16.0
    second = (rest * 64.0).astype(jnp.float16)
    rest = rest - second.astype(jnp.float32) / 64.0
    third = (rest * 16384.0).astype(jnp.float16)
    values = [power.astype(jnp.float16), first, second, third]
    tail = jnp.stack([values[min(i, 3)] for i in range(8)])
    tail = jnp.broadcast_to(tail[:, None], (8, lanes))
    small = jnp.concatenate([small, tail], axis=0)
    here = swap_blocks(jnp.broadcast_to(small, (count,) + small.shape), same_core_group)
    there = take_from(here, flip=1)
    grad_w, loss = assemble(place, here.astype(jnp.float32), there.astype(jnp.float32))
    return grad_w, loss[0, 0]


def body(features, proj_weight, image_vals, image_scales, text_vals, text_scales, logit_scale):
    rows = features.shape[0]
    total = rows * lax.axis_size("row") * lax.axis_size("col")
    place = (lax.axis_index("row") % 2).astype(jnp.int32).reshape(1)

    own = unit_targets(image_vals, image_scales, text_vals, text_scales)
    targets = gather_targets(own)
    tile, proj, points = project(gather_points(features), proj_weight)
    turned = tile.T
    first, near_cols, diag, *old = logits_of(points, logit_scale, targets[0], (), ())
    second, far_cols, *old = logits_of(points, logit_scale, targets[1], old, ())
    third, _, rows_part, cols_part = logits_of(
        points, logit_scale, targets[2], old, (near_cols, far_cols)
    )
    row_lse, col_lse = exchange_statistics(rows_part, cols_part)
    kept, sent, losses = grad_of(
        place,
        logit_scale,
        (first, second, third),
        sum(targets, []),
        row_lse,
        col_lse,
        diag,
        proj,
        turned,
    )
    grad_w, loss = total_sum(place, kept, sent, jnp.sum(losses[0]) * LN2)
    return (loss / (4.0 * total), grad_w)


def solution(mesh):
    return jax.shard_map(
        body,
        mesh=mesh,
        in_specs=(
            P(("row", "col"), None),
            P(),
            P(("row", "col"), None),
            P(("row", "col"), None),
            P(("row", "col"), None),
            P(("row", "col"), None),
            P(),
        ),
        out_specs=(P(), P()),
        check_vma=False,
    )
```

```python
import functools
import jax
import jax.numpy as jnp
from jax import lax
from jax.experimental import pallas as pl
from jax.experimental.pallas import tpu as pltpu
from jax.sharding import PartitionSpec as P

EPS = 1e-06
LOG2E = 1.4426950408889634
LN2 = 0.6931471805599453
SAFE = 60.0
AXES = ("row", "col")
X_POINT = (1, 0, 3, 2)
X_TARGET = (3, 2, 1, 0)
LANES = 128
WIDE = 2 * LANES
BATCHES = (((0, 0), (1, 0), (0, 1), (0, 3)), ((1, 3), (0, 2), (1, 1)), ((1, 2),))
ORDER = [(core,) + place for batch in BATCHES for core in range(2) for place in batch]
POINT_ORDER = (0, 1, 3, 4, 2, 5, 7, 6)


def device_index(x, y, z, core):
    row = ((x % 2) * 4 + y % 4) * 2 + core
    col = (x // 2) * 4 + z % 4
    return row * 8 + col


def take_from(value, x_map=None, dy=0, dz=0, flip=0):
    perm = []
    for x in range(4):
        source_x = x if x_map is None else x_map[x]
        for y in range(4):
            for z in range(4):
                for core in range(2):
                    source = device_index(source_x, y + dy, z + dz, core ^ flip)
                    perm.append((source, device_index(x, y, z, core)))
    return lax.ppermute(value, AXES, perm)


def whole():
    return pl.BlockSpec(memory_space=pltpu.VMEM)


def scalars():
    return pl.BlockSpec(memory_space=pltpu.SMEM)


def anywhere():
    return pl.BlockSpec(memory_space=pl.ANY)


def params(mib, grid=False):
    return pltpu.CompilerParams(
        vmem_limit_bytes=mib * 2**20, **({"dimension_semantics": ("arbitrary",)} if grid else {})
    )


def canonical(block):
    core, flip, step = block
    return (core * 2 + flip) * 4 + step


def unit_kernel(image_ref, image_scale_ref, text_ref, text_scale_ref, out_ref):
    count, width = image_ref.shape
    blocks = image_scale_ref.shape[0]
    size = width // blocks
    for which, (vals, scales_ref) in enumerate(
        ((image_ref, image_scale_ref), (text_ref, text_scale_ref))
    ):
        scales = scales_ref[...].astype(jnp.float32)
        scales = jnp.concatenate([scales] * (count // blocks), axis=0).T
        full = [
            vals[:, k * size : (k + 1) * size].astype(jnp.float32) * scales[:, k : k + 1]
            for k in range(blocks)
        ]
        square = sum(jnp.sum(part * part, axis=-1, keepdims=True) for part in full)
        inv = lax.rsqrt(square + EPS)
        for k in range(blocks):
            out_ref[which * count : (which + 1) * count, k * size : (k + 1) * size] = (
                full[k] * inv
            ).astype(jnp.bfloat16)


def unit_targets(image_vals, image_scales, text_vals, text_scales):
    count, width = image_vals.shape
    return pl.pallas_call(
        unit_kernel,
        out_shape=jax.ShapeDtypeStruct((2 * count, width), jnp.bfloat16),
        in_specs=[whole()] * 4,
        out_specs=whole(),
        compiler_params=params(58),
        cost_estimate=pl.CostEstimate(flops=2**20, bytes_accessed=2**20, transcendentals=0),
    )(image_vals, image_scales.T, text_vals, text_scales.T)


def proj_kernel(*refs):
    feature_refs = refs[:4]
    weight_ref = refs[4]
    outs, (tile_ref, weight_in_ref, proj_ref, unit_ref, in_sem, out_sem) = refs[-9:-6], refs[-6:]
    base = 0 if len(refs) == 14 else tile_ref.shape[0]
    rows = feature_refs[0].shape[0]
    step = 2 * rows
    incoming = [pltpu.make_async_copy(weight_ref, weight_in_ref, in_sem.at[4])]
    for k in range(4):
        to = tile_ref.at[k * rows : (k + 1) * rows, :]
        incoming.append(pltpu.make_async_copy(feature_refs[k], to, in_sem.at[k]))
    for copy in incoming:
        copy.start()
    for copy in incoming:
        copy.wait()
    outgoing = []

    def send(held_ref, out_ref, at, count):
        copy = pltpu.make_async_copy(
            held_ref.at[at : at + count, :],
            out_ref.at[base + at : base + at + count, :],
            out_sem.at[len(outgoing)],
        )
        copy.start()
        outgoing.append(copy)

    send(tile_ref, outs[0], 0, 2 * step)
    for at in range(0, 2 * step, step):
        proj = jnp.dot(
            tile_ref[at : at + step, :], weight_in_ref[...], preferred_element_type=jnp.float32
        )
        inv = lax.rsqrt(jnp.sum(proj * proj, axis=-1, keepdims=True) + EPS)
        proj_ref[at : at + step, :] = proj
        unit_ref[at : at + step, :] = (proj * inv).astype(jnp.bfloat16)
        send(proj_ref, outs[1], at, step)
        send(unit_ref, outs[2], at, step)
    for copy in outgoing:
        copy.wait()


def project(features, weight, done):
    deep, width = weight.shape
    rows = 4 * features[0].shape[0]
    return pl.pallas_call(
        proj_kernel,
        out_shape=(
            jax.ShapeDtypeStruct((2 * rows, deep), jnp.bfloat16),
            jax.ShapeDtypeStruct((2 * rows, width), jnp.float32),
            jax.ShapeDtypeStruct((2 * rows, width), jnp.bfloat16),
        ),
        in_specs=[anywhere()] * (5 + len(done)),
        out_specs=(anywhere(), anywhere(), anywhere()),
        input_output_aliases={5 + k: k for k in range(len(done))},
        scratch_shapes=[
            pltpu.VMEM((rows, deep), jnp.bfloat16),
            pltpu.VMEM((deep, width), jnp.bfloat16),
            pltpu.VMEM((rows, width), jnp.float32),
            pltpu.VMEM((rows, width), jnp.bfloat16),
            pltpu.SemaphoreType.DMA((5,)),
            pltpu.SemaphoreType.DMA((5,)),
        ],
        compiler_params=params(58),
        cost_estimate=pl.CostEstimate(
            flops=2 * rows * deep * width, bytes_accessed=6 * 2**20, transcendentals=0
        ),
    )(*features, weight, *done)


def to_column(row):
    parts = []
    for at in range(0, row.shape[1], LANES):
        wide = jnp.broadcast_to(row[:, at : at + LANES], (LANES, LANES))
        parts.append(wide.T)
    return jnp.concatenate(parts, axis=0)


def logits_kernel(count, first, last, *refs):
    refs = list(refs)
    scale_ref, points_ref = refs[:2]
    target_refs = refs[2 : 2 + count]
    refs = refs[2 + count :]
    if not first:
        old_max_ref, old_sum_ref = refs[:2]
        refs = refs[2:]
    if last:
        old_col_refs = refs[:1]
        refs = refs[1:]
    logits_ref, col_ref = refs[:2]
    refs = refs[2:]
    if first:
        diag_ref = refs.pop(0)
    if last:
        row_ref, all_col_ref = refs[:2]
        refs = refs[2:]
    row_max_ref, row_sum_ref, held_ref, col_max_ref, sem_ref = refs
    rows = points_ref.shape[0]
    chunk = 64
    scale = scale_ref[0] * LOG2E

    def copy_out(j):
        at = slice(j * WIDE, (j + 1) * WIDE)
        return pltpu.make_async_copy(held_ref.at[:, at], logits_ref.at[:, at], sem_ref.at[j])

    for j in range(count):
        at = slice(j * WIDE, (j + 1) * WIDE)
        held_ref[:, at] = scale * lax.dot_general(
            points_ref[...],
            target_refs[j][...],
            (((1,), (1,)), ((), ())),
            preferred_element_type=jnp.float32,
        )
        copy_out(j).start()
        top = None
        for r in range(0, rows, chunk):
            value = held_ref[r : r + chunk, at]
            if j:
                row_max_ref[r : r + chunk, :] = jnp.maximum(row_max_ref[r : r + chunk, :], value)
            elif first:
                row_max_ref[r : r + chunk, :] = value
            else:
                row_max_ref[r : r + chunk, :] = jnp.maximum(old_max_ref[r : r + chunk, :], value)
            part = jnp.max(value.reshape(chunk // 8, 8, WIDE), axis=0)
            top = part if top is None else jnp.maximum(top, part)
        col_max_ref[j : j + 1, :] = jnp.max(top, axis=0, keepdims=True)

    if first:
        rows_at = lax.broadcasted_iota(jnp.int32, (LANES, WIDE), 0)
        cols_at = lax.broadcasted_iota(jnp.int32, (LANES, WIDE), 1) % LANES
        own = jnp.where(rows_at == cols_at, held_ref[:LANES, :WIDE], 0.0)
        diag_ref[...] = jnp.broadcast_to(jnp.sum(own, axis=0, keepdims=True), diag_ref.shape)
        row_sum_ref[...] = jnp.zeros(row_sum_ref.shape, jnp.float32)
    else:
        row_sum_ref[...] = old_sum_ref[...] * jnp.exp2(old_max_ref[...] - row_max_ref[...])

    def sums(j, _):
        at = pl.ds(pl.multiple_of(j * WIDE, WIDE), WIDE)
        top = col_max_ref[pl.ds(j, 1), :]
        total = jnp.zeros((8, WIDE), jnp.float32)
        for r in range(0, rows, chunk):
            value = held_ref[r : r + chunk, at]
            row_sum_ref[r : r + chunk, :] += jnp.exp2(value - row_max_ref[r : r + chunk, :])
            total += jnp.sum(jnp.exp2(value - top).reshape(chunk // 8, 8, WIDE), axis=0)
        col_ref[pl.ds(j, 1), :] = top + jnp.log(jnp.sum(total, axis=0, keepdims=True)) * LOG2E
        return 0

    lax.fori_loop(0, count, sums, 0)
    if last:
        k = 0
        for source in (*old_col_refs, col_ref):
            for at in range(source.shape[0]):
                to = canonical(ORDER[k])
                all_col_ref[to : to + 1, :] = source[at : at + 1, :]
                k += 1
        for which in range(2):
            lanes = slice(which * LANES, (which + 1) * LANES)
            for r in range(0, rows, LANES):
                tops = row_max_ref[r : r + LANES, lanes].T
                part = row_sum_ref[r : r + LANES, lanes].T
                top = jnp.max(tops, axis=0, keepdims=True)
                total = jnp.sum(part * jnp.exp2(tops - top), axis=0, keepdims=True)
                to = POINT_ORDER[r // LANES] * LANES
                row_ref[which : which + 1, to : to + LANES] = top + jnp.log(total) * LOG2E
    for j in range(count):
        copy_out(j).wait()


def logits_of(points, scale, targets, old, old_cols):
    rows = points.shape[0]
    count = len(targets)
    cols = count * WIDE
    first, last = not old, bool(old_cols)
    lanes = jax.ShapeDtypeStruct((rows, WIDE), jnp.float32)
    held = [pltpu.VMEM(lanes.shape, jnp.float32)] * 2
    outs = [
        jax.ShapeDtypeStruct((rows, cols), jnp.float32),
        jax.ShapeDtypeStruct((count, WIDE), jnp.float32),
    ]
    if first:
        outs.append(jax.ShapeDtypeStruct((8, WIDE), jnp.float32))
    if last:
        outs.append(jax.ShapeDtypeStruct((2, rows), jnp.float32))
        outs.append(jax.ShapeDtypeStruct((16, WIDE), jnp.float32))
    else:
        outs += [lanes, lanes]
    return pl.pallas_call(
        functools.partial(logits_kernel, count, first, last),
        out_shape=outs,
        in_specs=[scalars()] + [whole()] * (1 + count + len(old) + len(old_cols)),
        out_specs=[pl.BlockSpec(memory_space=pl.ANY)] + [whole()] * (len(outs) - 1),
        scratch_shapes=(held if last else [])
        + [
            pltpu.VMEM((rows, cols), jnp.float32),
            pltpu.VMEM((count, WIDE), jnp.float32),
            pltpu.SemaphoreType.DMA((count,)),
        ],
        compiler_params=params(58),
        cost_estimate=pl.CostEstimate(
            flops=2 * rows * cols * points.shape[1],
            bytes_accessed=4 * rows * cols,
            transcendentals=2 * rows * cols,
        ),
    )(scale, points, *targets, *old, *old_cols)


def grad_kernel(place_ref, scale_ref, *refs):
    logits_refs = refs[:2]
    target_refs = refs[2:18]
    row_ref, all_col_ref, diag_ref, proj_ref, turned_any, kept_ref, sent_ref, loss_ref = refs[18:26]
    coef_ref, targets_ref, tops_ref, shares_ref, edges_ref, high_ref, low_ref = refs[26:33]
    part_ref, turned_ref, sem_ref = refs[33:]
    step = pl.program_id(0)
    size = proj_ref.shape[0]
    scale = scale_ref[0]
    chunk = 64

    def copy_in(k):
        if k == 16:
            return pltpu.make_async_copy(turned_any, turned_ref, sem_ref.at[k])
        return pltpu.make_async_copy(
            target_refs[k], targets_ref.at[k * WIDE : (k + 1) * WIDE, :], sem_ref.at[k]
        )

    peak = jnp.max(row_ref[...])
    near = peak - jnp.min(all_col_ref[...]) < SAFE

    @pl.when(step == 0)
    def _():
        for k in range(16):
            copy_in(k).start()
        for k, block in enumerate(ORDER):
            at = canonical(block)
            edges_ref[k : k + 1, :] = all_col_ref[at : at + 1, :]
        for k, place in enumerate(POINT_ORDER):
            for which in range(2):
                row = row_ref[which : which + 1, place * LANES : (place + 1) * LANES]
                r_at = slice(k * LANES, (k + 1) * LANES)
                lanes = slice(which * LANES, (which + 1) * LANES)
                tops_ref[r_at, lanes] = to_column(row)
                shares_ref[r_at, lanes] = to_column(jnp.exp2(row - peak))
        both = edges_ref[:1, :] - 2.0 * diag_ref[:1, :]
        both = both[:, :LANES] + both[:, LANES:] + row_ref[:1, :LANES] + row_ref[1:2, :LANES]
        loss_ref[...] = jnp.broadcast_to(both, loss_ref.shape)

    @pl.when(step == 1)
    def _():
        copy_in(16).start()

    def own_hits(r):
        rows_at = lax.broadcasted_iota(jnp.int32, (chunk, WIDE), 0) + r + step * size
        cols_at = lax.broadcasted_iota(jnp.int32, (chunk, WIDE), 1) % LANES
        return jnp.where(rows_at == cols_at, 2.0, 0.0)

    def coefs(is_near):
        k = 0
        for logits_ref in logits_refs:
            for at in range(0, logits_ref.shape[1], WIDE):
                edge = edges_ref[k : k + 1, :]
                rise = jnp.exp2(peak - edge)
                for r in range(0, size, chunk):
                    value = logits_ref[r : r + chunk, at : at + WIDE]
                    r_at = pl.ds(pl.multiple_of(step * size + r, chunk), chunk)
                    coef = jnp.exp2(value - tops_ref[r_at, :])
                    if is_near:
                        coef = coef + coef * (shares_ref[r_at, :] * rise)
                    else:
                        coef = coef + jnp.exp2(value - edge)
                    if k == 0 and r < LANES:
                        coef = coef - own_hits(r)
                    coef_ref[r : r + chunk, k * WIDE : (k + 1) * WIDE] = coef.astype(jnp.bfloat16)
                k += 1

    @pl.when(near)
    def _():
        coefs(True)

    @pl.when(jnp.logical_not(near))
    def _():
        coefs(False)

    @pl.when(step == 0)
    def _():
        for k in range(16):
            copy_in(k).wait()

    grad = jnp.dot(coef_ref[...], targets_ref[...], preferred_element_type=jnp.float32)
    grad = grad * (scale * 0.25)
    proj = proj_ref[...]
    inv = lax.rsqrt(jnp.sum(proj * proj, axis=-1, keepdims=True) + EPS)
    along = jnp.sum(proj * grad, axis=-1, keepdims=True)
    grad = inv * (grad - along * inv * inv * proj)
    high = grad.astype(jnp.bfloat16)
    rows = pl.ds(pl.multiple_of(step * size, size), size)
    high_ref[rows, :] = high
    low_ref[rows, :] = (grad - high.astype(jnp.float32)).astype(jnp.bfloat16)

    @pl.when(step == pl.num_programs(0) - 1)
    def _():
        copy_in(16).wait()
        core = place_ref[0]
        deep = turned_ref.shape[0]
        cut = deep // 16

        def products(n, _):
            at = pl.ds(pl.multiple_of(n * WIDE, WIDE), WIDE)
            part_ref[...] = jnp.dot(
                turned_ref[...], high_ref[:, at], preferred_element_type=jnp.float32
            ) + jnp.dot(turned_ref[...], low_ref[:, at], preferred_element_type=jnp.float32)
            for v in range(8):
                for side in range(2):
                    lanes = slice(side * LANES, (side + 1) * LANES)
                    for out_ref, half in ((kept_ref, core), (sent_ref, 1 - core)):
                        from_row = pl.multiple_of(half * (deep // 2) + v * cut, 8)
                        out_ref[v * 8 + 2 * n + side] = part_ref[pl.ds(from_row, cut), lanes]
            return 0

        lax.fori_loop(0, high_ref.shape[1] // WIDE, products, 0)


def grad_of(place, scale, logits, targets, row_lse, col_lse, diag, proj, turned):
    rows, width = proj.shape
    deep = turned.shape[0]
    step = 256
    cut = deep // 16
    piece = jax.ShapeDtypeStruct((64, cut, LANES), jnp.float32)
    cols = sum(part.shape[1] for part in logits)
    return pl.pallas_call(
        grad_kernel,
        grid=(rows // step,),
        out_shape=(piece, piece, jax.ShapeDtypeStruct((8, LANES), jnp.float32)),
        in_specs=[scalars(), scalars()]
        + [pl.BlockSpec((step, part.shape[1]), lambda i: (i, 0)) for part in logits]
        + [anywhere()] * len(targets)
        + [whole(), whole(), whole()]
        + [pl.BlockSpec((step, width), lambda i: (i, 0)), anywhere()],
        out_specs=(whole(), whole(), whole()),
        scratch_shapes=[
            pltpu.VMEM((step, cols), jnp.bfloat16),
            pltpu.VMEM((cols, width), jnp.bfloat16),
            pltpu.VMEM((rows, WIDE), jnp.float32),
            pltpu.VMEM((rows, WIDE), jnp.float32),
            pltpu.VMEM((16, WIDE), jnp.float32),
            pltpu.VMEM((rows, width), jnp.bfloat16),
            pltpu.VMEM((rows, width), jnp.bfloat16),
            pltpu.VMEM((deep, WIDE), jnp.float32),
            pltpu.VMEM((deep, rows), jnp.bfloat16),
            pltpu.SemaphoreType.DMA((len(targets) + 1,)),
        ],
        compiler_params=params(58, True),
        cost_estimate=pl.CostEstimate(
            flops=2 * rows * cols * width, bytes_accessed=32 * 2**20, transcendentals=rows * cols
        ),
    )(place, scale, *logits, *targets, row_lse, col_lse, diag, proj, turned)


def assemble_kernel(place_ref, here_ref, there_ref, out_ref, loss_ref, held_ref, sem_ref):
    cut = here_ref.shape[1] - 8
    half = 8 * cut
    copies = []
    loss = jnp.zeros((1, LANES), jnp.float32)
    for turn, ref in enumerate((here_ref, there_ref)):
        from_row = pl.multiple_of((place_ref[0] ^ turn) * half, 8)
        for v in range(8):
            for w in range(8):
                flags = [ref[v * 8 + w, cut + k : cut + k + 1, :] for k in range(4)]
                held_ref[turn, v * cut : (v + 1) * cut, w * LANES : (w + 1) * LANES] = ref[
                    v * 8 + w, :cut
                ] * jnp.exp2(-flags[0])
                loss += flags[1] * 16.0 + flags[2] / 64.0 + flags[3] / 16384.0
        copy = pltpu.make_async_copy(
            held_ref.at[turn], out_ref.at[pl.ds(from_row, half), :], sem_ref.at[turn]
        )
        copy.start()
        copies.append(copy)
    loss_ref[...] = jnp.broadcast_to(loss, loss_ref.shape)
    for copy in copies:
        copy.wait()


def assemble(place, here, there):
    cut = here.shape[1] - 8
    return pl.pallas_call(
        assemble_kernel,
        in_specs=[scalars(), whole(), whole()],
        out_specs=(anywhere(), whole()),
        out_shape=(
            jax.ShapeDtypeStruct((16 * cut, 8 * LANES), jnp.float32),
            jax.ShapeDtypeStruct((8, LANES), jnp.float32),
        ),
        scratch_shapes=[
            pltpu.VMEM((2, 8 * cut, 8 * LANES), jnp.float32),
            pltpu.SemaphoreType.DMA((2,)),
        ],
        compiler_params=params(16),
        cost_estimate=pl.CostEstimate(flops=2**20, bytes_accessed=9 * 2**20, transcendentals=0),
    )(place, here, there)


def same_core_group(x, y, z, core):
    return (core,), (x, y, z)


def groups_of(rule):
    found = {}
    for x in range(4):
        for y in range(4):
            for z in range(4):
                for core in range(2):
                    group, place = rule(x, y, z, core)
                    found.setdefault(group, []).append((place, device_index(x, y, z, core)))
    return [[device for _, device in sorted(found[group])] for group in sorted(found)]


def swap_blocks(value, rule):
    return lax.all_to_all(
        value, AXES, split_axis=0, concat_axis=0, axis_index_groups=groups_of(rule), tiled=True
    )


def merged(value, got):
    low, high = jnp.minimum(value, got), jnp.maximum(value, got)
    return high + jnp.log(1.0 + jnp.exp2(low - high)) * LOG2E


def exchange_statistics(rows, cols):
    row_shape = (2, 2, 4, rows.shape[1] // 8)
    col_shape = (2, 2, 4, cols.shape[1])

    def row_add(value, got):
        return merged(value, got.reshape(rows.shape))

    def col_add(value, got):
        return merged(value, got.reshape(cols.shape))

    got_rows = take_from(rows, x_map=X_POINT)
    got_cols = take_from(cols, flip=1)
    rows = row_add(rows, got_rows.reshape(row_shape)[:, ::-1])
    cols = col_add(cols, got_cols.reshape(col_shape)[::-1])
    rows, cols = lax.optimization_barrier((rows, cols))
    got_rows = take_from(rows, dz=1)
    got_cols = take_from(cols, x_map=X_TARGET)
    rows = row_add(rows, jnp.roll(got_rows.reshape(row_shape), 1, axis=2))
    cols = col_add(cols, got_cols.reshape(col_shape)[:, ::-1])
    rows, cols = lax.optimization_barrier((rows, cols))
    got_rows = take_from(rows, dz=2)
    got_cols = take_from(cols, dy=1)
    rows = row_add(rows, jnp.roll(got_rows.reshape(row_shape), 2, axis=2))
    cols = col_add(cols, jnp.roll(got_cols.reshape(col_shape), 1, axis=2))
    got_cols = take_from(cols, dy=2)
    return rows, col_add(cols, jnp.roll(got_cols.reshape(col_shape), 2, axis=2))


def gather_and_project(own_points, own_targets, weight):
    def near_point(value):
        return take_from(value, x_map=X_POINT)

    def near_target(value):
        return take_from(value, x_map=X_TARGET)

    own = own_points
    beside, after, before = near_point(own), take_from(own, dz=1), take_from(own, dz=-1)
    target = own_targets
    near = [own, after, before, beside]
    beside_after, far = near_point(after), take_from(after, dz=1)
    beside_before = take_from(beside, dz=-1)
    t_beside, t_after = near_target(target), take_from(target, dy=1)

    t_before = take_from(target, dy=-1)
    beside_far = take_from(beside_after, dz=1)
    half = project(near, weight, ())
    t_beside, t_after, far, beside_before, beside_far, half = lax.optimization_barrier(
        (t_beside, t_after, far, beside_before, beside_far, half)
    )
    t_beside_after, t_far = near_target(t_after), take_from(t_after, dy=1)
    t_beside_before = take_from(t_beside, dy=-1)
    points = project([far, beside_after, beside_before, beside_far], weight, half)
    first = [target, t_beside, t_after, t_before]
    return points, first, [t_beside_before, t_far, t_beside_after]


def with_other(blocks):
    return blocks + [take_from(block, flip=1) for block in blocks]


def total_sum(place, kept, sent, local_loss):
    count, cut, lanes = kept.shape
    half = kept + take_from(sent, flip=1)
    own = jnp.sum(swap_blocks(half, same_core_group), axis=0)
    power = 14.0 - jnp.floor(jnp.log2(jnp.maximum(jnp.max(jnp.abs(own)), 1e-30)))
    small = (own * jnp.exp2(power)).astype(jnp.float16)
    first = (local_loss / 16.0).astype(jnp.float16)
    rest = local_loss - first.astype(jnp.float32) * 16.0
    second = (rest * 64.0).astype(jnp.float16)
    rest = rest - second.astype(jnp.float32) / 64.0
    third = (rest * 16384.0).astype(jnp.float16)
    values = [power.astype(jnp.float16), first, second, third]
    tail = jnp.stack([values[min(i, 3)] for i in range(8)])
    tail = jnp.broadcast_to(tail[:, None], (8, lanes))
    small = jnp.concatenate([small, tail], axis=0)
    here = swap_blocks(jnp.broadcast_to(small, (count,) + small.shape), same_core_group)
    there = take_from(here, flip=1)
    grad_w, loss = assemble(place, here.astype(jnp.float32), there.astype(jnp.float32))
    return grad_w, loss[0, 0]


def body(features, proj_weight, image_vals, image_scales, text_vals, text_scales, logit_scale):
    rows = features.shape[0]
    total = rows * lax.axis_size("row") * lax.axis_size("col")
    place = (lax.axis_index("row") % 2).astype(jnp.int32).reshape(1)

    own = unit_targets(image_vals, image_scales, text_vals, text_scales)
    (tile, proj, points), near, far = gather_and_project(features, own, proj_weight)
    turned = tile.T
    near = with_other(near)
    beside_after, points = lax.optimization_barrier((far[-1], points))
    last = take_from(beside_after, dy=1)
    far = with_other(far)
    first, near_cols, diag, *old = logits_of(points, logit_scale, near, (), ())
    last, near_cols = lax.optimization_barrier((last, near_cols))
    far = far + with_other([last])
    second, _, rows_part, cols_part = logits_of(points, logit_scale, far, old, (near_cols,))
    row_lse, col_lse = exchange_statistics(rows_part, cols_part)
    kept, sent, losses = grad_of(
        place,
        logit_scale,
        (first, second),
        near + far,
        row_lse,
        col_lse,
        diag,
        proj,
        turned,
    )
    grad_w, loss = total_sum(place, kept, sent, jnp.sum(losses[0]) * LN2)
    return (loss / (4.0 * total), grad_w)


def solution(mesh):
    return jax.shard_map(
        body,
        mesh=mesh,
        in_specs=(
            P(("row", "col"), None),
            P(),
            P(("row", "col"), None),
            P(("row", "col"), None),
            P(("row", "col"), None),
            P(("row", "col"), None),
            P(),
        ),
        out_specs=(P(), P()),
        check_vma=False,
    )
```
